32 devices in a mesh: tile: 16 (over z, x, core), row: 2 (over y).
Axes of the slice: x: 2, y: 2, z: 4, core: 2. Of those that a mesh axis runs over, the one named last changes fastest.
Arguments:
- swath_blocks: bfloat16 [16, 2, 768, 2048], P('tile', 'row'), may hold values from -6 to 6
- footprint: int32 [16, 2, 768, 1], P('tile', 'row'), may hold values from 0 to 31; in each aligned block of 768 rows (0 to 767, 768 to 1535, ..., all dimensions but the last counted through in order) at most 36 rows name the same one
- cell_row: int32 [16, 2, 768], P('tile', 'row'), may hold values from 0 to 127
- tile_pick: int32 [16, 2, 768], P('tile', 'row'), may hold values from 0 to 3
- sensor: int32 [16, 2, 768], P('tile', 'row'), may hold values from 0 to 1
- bandpass_offset: float32 [2, 8, 8], replicated, may hold values from -0.4 to 0.4
- weight_tiles: bfloat16 [4, 256, 256], replicated, may hold values from -0.375 to 0.375
- lookup_table: float32 [8, 33], replicated, may hold values from 0.5 to 2
- lookup_bin: int32 [16, 256, 256], P('tile', 'row'), may hold values from 0 to 31
- lookup_frac: float32 [16, 256, 256], P('tile', 'row'), may hold values from 0 to 1
- brdf_params: float32 [8, 3], replicated, may hold values from 0.05 to 1
- vol_kernel: float32 [16, 256, 256], P('tile', 'row'), may hold values from 0.1 to 2
- geo_kernel: float32 [16, 256, 256], P('tile', 'row'), may hold values from 0.1 to 2
- clear_mask: int32 [16, 256, 256], P('tile', 'row'), may hold values 0 or 1
Outputs:
- nbar: bfloat16 [16, 256, 2048], P('tile', 'row')
The draws below stay inside these ranges and needn't reach their ends.
Inputs may be any that keep to these rules, and one draw needn't show every extreme that they name: `footprint`: at most 36 of the blocks of one device name one destination, and in every draw some destination is named by exactly 36 of them.
All inputs are finite; a program needn't handle non-finite values. No bound on the sum of `clear_mask` on one device may be relied on, other than what follows from the above.
Results may differ from the reference program's by a relative error of at most 0.0057.
Values may be sent and summed in bfloat16 or wider, within the bound.
No kernel may reach another device: no remote copies, remote signals or barrier semaphores. Data moves between devices by JAX's collectives and lax.ppermute only.
A program may use at most 64 MiB of HBM per device.

```python
import math
import jax
import jax.numpy as jnp
import numpy as np
from jax import lax

BANDS = 8
BPIX = 256
KT = 4
NBIN = 32
SB = 768
NCB = 128
DESTS = 32
CAP = 36
GR = 256
N_TILE = 16
N_ROW = 2


def with_ends(array, rng, least, top_value):
    shape = array.shape
    place = [jax.random.randint(jax.random.fold_in(rng, axis), (), 0, shape[axis]) for axis in range(len(shape))]
    array = array.at[tuple(place)].set(least)
    longest = shape.index(max(shape))
    place[longest] = (place[longest] + 1) % shape[longest]
    return array.at[tuple(place)].set(top_value)


def block_levels(own_key, shape, cuts, smallest, largest):
    factor_of, own = 1.0, jax.random.fold_in(own_key, 6)
    for axis_at, parts in cuts:
        steps = jnp.exp(jax.random.uniform(jax.random.fold_in(own, axis_at), (parts,), jnp.float32, smallest / len(cuts), largest / len(cuts)))
        factor_of = factor_of * jnp.repeat(steps, shape[axis_at] // parts).reshape([-1 if axis == axis_at else 1 for axis in range(len(shape))])
    return factor_of


def routed_block(rng, own, number, rows, amount, top, limit, slope):
    order = jax.random.permutation(rng, amount)
    crowded, ordinary = load_shares(amount, rows * top, limit, slope, True), load_shares(amount, rows * top, limit, slope, False)
    places = jnp.arange(amount)

    def named(lengths, turn):
        used = int((lengths > 0).sum())
        fixed = max(1, used // 4)
        passed = fixed + (places - fixed + turn * (used - fixed)) % max(1, amount - fixed)
        return jnp.zeros((amount,), jnp.int32).at[order[jnp.where(places < fixed, places, passed)]].set(jnp.asarray(lengths, jnp.int32))

    lengths = jnp.where(number % 4 == 0, named(crowded, number // 4), named(ordinary, number - number // 4 - 1))
    mixed = jax.random.permutation(jax.random.fold_in(own, 3), amount)
    giver, taker = mixed[0:amount // 2 * 2:2], mixed[1:amount // 2 * 2:2]
    room = jnp.minimum(lengths[giver] - 1, limit - lengths[taker]) // 2
    room = jnp.where((giver == order[0]) | (taker == order[0]) | (lengths[taker] == 0), 0, jnp.maximum(room, 0))
    passed = jax.random.randint(jax.random.fold_in(own, 4), (amount // 2,), 0, 1 << 20) % (room + 1)
    lengths = lengths.at[giver].add(-passed).at[taker].add(passed)
    labels = jnp.searchsorted(jnp.cumsum(lengths), jnp.arange(rows * top), side="right").astype(jnp.int32)
    listing = labels.reshape(top, rows).T
    listing = listing[jax.random.permutation(jax.random.fold_in(own, 1), rows)]
    turn = jax.random.randint(jax.random.fold_in(own, 2), (rows, 1), 0, top)
    return jnp.take_along_axis(listing, (jnp.arange(top)[None, :] + turn) % top, axis=1)


def load_shares(amount, total, bound, lean, full):
    portions = [(1 << 20) // math.isqrt(rank ** lean) + 1 for rank in range(1, amount + 1)]
    largest = bound if full else min(bound, max(-(-total // amount), total * portions[0] // sum(portions)))
    least = 1 if total - largest >= amount - 1 else 0
    counts, rest = [largest] + [least] * (amount - 1), total - largest - least * (amount - 1)
    while rest > 0:
        movable = [i for i in range(1, amount) if counts[i] < largest] or [i for i in range(1, amount) if counts[i] < bound]
        whole, left = sum([portions[i] for i in movable]), rest
        for i in movable:
            extra = min(bound - counts[i], max(1, left * portions[i] // whole), rest)
            counts[i] = counts[i] + extra
            rest = rest - extra
    return np.array(counts)


def bell_draw(stream_key, dims, deviation, reach, shards=(), kind=jnp.bfloat16):
    array = deviation * jax.random.normal(stream_key, dims, jnp.float32)
    if shards:
        array = array * block_levels(stream_key, dims, shards, -0.22, 0.18)
    return jnp.clip(array, -reach, reach).astype(kind)


def setup_inputs(seed: int = 0) -> dict:
    arg_keys = jax.random.split(jax.random.key(seed), 15)
    swath_blocks = bell_draw(arg_keys[0], (N_TILE, N_ROW, SB, BANDS * BPIX), 1.0, 6.0, ((0, 16), (1, 2)))
    footprint_keys = jax.random.split(jax.random.fold_in(arg_keys[1], 1), N_TILE * N_ROW * SB // SB)
    footprint_turns = jax.random.permutation(jax.random.fold_in(arg_keys[1], 3), N_TILE * N_ROW * SB // SB)
    footprint = jax.vmap(lambda own, number: routed_block(jax.random.fold_in(arg_keys[1], 2), own, number, SB, DESTS, 1, CAP, 2))(footprint_keys, footprint_turns).reshape((N_TILE, N_ROW, SB, 1))
    cell_row = with_ends(jax.random.randint(arg_keys[2], (N_TILE, N_ROW, SB), 0, NCB), jax.random.fold_in(arg_keys[2], 1), 0, NCB - 1).astype(jnp.int32)
    tile_pick = with_ends(jax.random.randint(arg_keys[3], (N_TILE, N_ROW, SB), 0, KT), jax.random.fold_in(arg_keys[3], 1), 0, KT - 1).astype(jnp.int32)
    sensor = with_ends(jax.random.randint(arg_keys[4], (N_TILE, N_ROW, SB), 0, 2), jax.random.fold_in(arg_keys[4], 1), 0, 1).astype(jnp.int32)
    bandpass_offset = jnp.clip(jax.random.uniform(arg_keys[5], (2, BANDS, BANDS), jnp.float32, -0.4, 0.4), -0.4, 0.4)
    weight_tiles = bell_draw(arg_keys[6], (KT, BPIX, BPIX), BPIX ** -0.5, 0.375)
    lookup_table = jnp.clip(jnp.exp(jax.random.uniform(arg_keys[7], (BANDS, NBIN + 1), jnp.float32, math.log(0.5), math.log(2.0))), 0.5, 2.0)
    lookup_bin = with_ends(jax.random.randint(arg_keys[8], (N_TILE, GR, BPIX), 0, NBIN), jax.random.fold_in(arg_keys[8], 1), 0, NBIN - 1).astype(jnp.int32)
    lookup_frac = jnp.clip(1.0 * jax.random.uniform(arg_keys[9], (N_TILE, GR, BPIX), jnp.float32) ** block_levels(arg_keys[9], (N_TILE, GR, BPIX), ((0, 16), (1, 2)), -0.2, 0.2), 0.0, 1.0)
    brdf_params = jnp.clip(jnp.exp(jax.random.uniform(arg_keys[10], (BANDS, 3), jnp.float32, math.log(0.05), math.log(1.0))), 0.05, 1.0)
    vol_kernel = jnp.clip(jnp.exp(math.log(2.0) - 2.9957323 * jax.random.uniform(arg_keys[11], (N_TILE, GR, BPIX), jnp.float32) ** block_levels(arg_keys[11], (N_TILE, GR, BPIX), ((0, 16), (1, 2)), -0.2, 0.2)), 0.1, 2.0)
    geo_kernel = jnp.clip(jnp.exp(math.log(2.0) - 2.9957323 * jax.random.uniform(arg_keys[12], (N_TILE, GR, BPIX), jnp.float32) ** block_levels(arg_keys[12], (N_TILE, GR, BPIX), ((0, 16), (1, 2)), -0.2, 0.2)), 0.1, 2.0)
    clear_mask = with_ends((jax.random.randint(arg_keys[13], (N_TILE, GR, BPIX), 0, 5) < 4).astype(jnp.int32), jax.random.fold_in(arg_keys[13], 1), 0, 1)
    return dict(swath_blocks=swath_blocks, footprint=footprint, cell_row=cell_row, tile_pick=tile_pick, sensor=sensor, bandpass_offset=bandpass_offset, weight_tiles=weight_tiles, lookup_table=lookup_table, lookup_bin=lookup_bin, lookup_frac=lookup_frac, brdf_params=brdf_params, vol_kernel=vol_kernel, geo_kernel=geo_kernel, clear_mask=clear_mask)


nadir_volume = 0.3
nadir_geometric = 0.6


def reference(swath_blocks, footprint, cell_row, tile_pick, sensor, bandpass_offset, weight_tiles, lookup_table, lookup_bin, lookup_frac, brdf_params, vol_kernel, geo_kernel, clear_mask):
    row_width = BANDS * BPIX
    mixing = jnp.eye(BANDS, dtype=jnp.float32)[None, :, :] + bandpass_offset
    stacked_weights = weight_tiles.reshape(KT * BPIX, BPIX)
    device_count = N_TILE * N_ROW
    xs = (swath_blocks.reshape(device_count, SB, row_width),
          footprint.reshape(device_count, SB),
          cell_row.reshape(device_count, SB),
          tile_pick.reshape(device_count, SB),
          sensor.reshape(device_count, SB))

    def add_group(accum_grid, operands):
        payload, target, rows_here, picks, sensors = operands
        chosen_mix = mixing[sensors]
        banded = jnp.einsum('sbc,scp->sbp', chosen_mix, payload.reshape(SB, BANDS, BPIX).astype(jnp.float32), precision=lax.Precision.HIGHEST).astype(jnp.bfloat16)
        chosen = picks[:, None] == jnp.arange(KT, dtype=jnp.int32)[None, :]
        spread = jnp.where(chosen[:, None, :, None], banded[:, :, None, :], jnp.zeros((), jnp.bfloat16))
        resampled = jnp.dot(spread.reshape(SB * BANDS, KT * BPIX), stacked_weights, preferred_element_type=jnp.float32).astype(jnp.bfloat16)
        tile_index = target // N_ROW
        grid_row = (target % N_ROW) * NCB + rows_here
        accum_grid = accum_grid.at[tile_index, grid_row].add(resampled.reshape(SB, row_width).astype(jnp.float32))
        return accum_grid, None

    accum_grid = jnp.zeros((N_TILE, GR, row_width), jnp.float32)
    accum_grid, unused = lax.scan(add_group, accum_grid, xs)
    padded = jnp.pad(accum_grid, ((0, 0), (1, 1), (0, 0)))
    smoothed = 0.25 * padded[:, :-2] + 0.5 * padded[:, 1:-1] + 0.25 * padded[:, 2:]
    smoothed = smoothed.reshape(N_TILE, GR, BANDS, BPIX)
    lower_value = jnp.moveaxis(lookup_table[:, lookup_bin], 0, 2)
    upper_value = jnp.moveaxis(lookup_table[:, lookup_bin + 1], 0, 2)
    fraction = lookup_frac[:, :, None, :]
    table_value = lower_value * (1.0 - fraction) + upper_value * fraction
    isotropic = brdf_params[:, 0][None, None, :, None]
    volume = brdf_params[:, 1][None, None, :, None]
    geometric = brdf_params[:, 2][None, None, :, None]
    numerator = isotropic + volume * nadir_volume + geometric * nadir_geometric
    denominator = isotropic + volume * vol_kernel[:, :, None, :] + geometric * geo_kernel[:, :, None, :]
    cfactor = numerator / denominator
    result = smoothed * table_value * cfactor * clear_mask[:, :, None, :].astype(jnp.float32)
    return result.reshape(N_TILE, GR, row_width).astype(jnp.bfloat16)
```

```python
import functools

import jax
import jax.numpy as jnp
from jax import lax
from jax.experimental import pallas as pl
from jax.experimental.pallas import tpu as pltpu
from jax.sharding import PartitionSpec as P

nadir_volume = 0.3
nadir_geometric = 0.6

GROUP = 32
CHUNKS = ((0, 3), (3, 6), (6, 8))
VMEM_LIMIT = 40 * 1024 * 1024


def params():
    return pltpu.CompilerParams(vmem_limit_bytes=VMEM_LIMIT)


def dot(a, b):
    return jnp.dot(a, b, preferred_element_type=jnp.float32)


def resample_kernel(bands, pixels, x_ref, sensor_ref, pick_ref, mix_ref, weights_ref, out_ref):
    tiles = weights_ref.shape[0]
    groups = x_ref.shape[0] // GROUP

    def one_group(g, carry):
        rows = pl.ds(pl.multiple_of(g * GROUP, GROUP), GROUP)
        block = x_ref[rows, :]
        stacked = jnp.concatenate(
            [block[:, c * pixels : (c + 1) * pixels] for c in range(bands)], axis=0
        )
        second = sensor_ref[g] == 1
        high = jnp.where(second, mix_ref[1, 0], mix_ref[0, 0])
        low = jnp.where(second, mix_ref[1, 1], mix_ref[0, 1])
        banded = (
            dot(high.astype(jnp.bfloat16), stacked) + dot(low.astype(jnp.bfloat16), stacked)
        )
        pick = jnp.concatenate([pick_ref[rows, :]] * bands, axis=0)
        total = jnp.zeros((bands * GROUP, pixels), jnp.float32)
        for t in range(tiles):
            masked = jnp.where(pick == t, banded, 0.0).astype(jnp.bfloat16)
            total = total + dot(masked, weights_ref[t])
        result = total.astype(jnp.bfloat16)
        for b in range(bands):
            out_ref[rows, b * pixels : (b + 1) * pixels] = result[b * GROUP : (b + 1) * GROUP]
        return carry

    lax.fori_loop(0, groups, one_group, 0)


def pack_kernel(position_ref, rows_ref, own_ref, other_ref):
    peers, slots, columns = own_ref.shape
    blocks = rows_ref.shape[0]
    position = position_ref[...]
    for half, ref in ((0, own_ref), (1, other_ref)):
        for k in range(peers):
            first = (half * peers + k) * slots
            ids = lax.broadcasted_iota(jnp.int32, (slots, blocks), 0) + first
            onehot = (ids == position).astype(jnp.float32).astype(jnp.bfloat16)
            ref[k] = dot(onehot, rows_ref[...]).astype(jnp.bfloat16)


def merge_kernel(count, cells, *refs):
    tags, rows = refs[:count], refs[count : 2 * count]
    own_ref, send_ref = refs[2 * count :]
    depth = send_ref.shape[0] + 1
    for d in range(depth):
        total = None
        for tag_ref, row_ref in zip(tags, rows):
            slots = row_ref.shape[0]
            ids = lax.broadcasted_iota(jnp.int32, (cells, slots), 0) + d * cells
            onehot = (ids == tag_ref[...]).astype(jnp.float32).astype(jnp.bfloat16)
            part = dot(onehot, row_ref[...])
            total = part if total is None else total + part
        if d == 0:
            own_ref[...] = total
        else:
            send_ref[d - 1] = total.astype(jnp.bfloat16)


def factor_kernel(bands, pixels, bin_ref, frac_ref, vol_ref, geo_ref, mask_ref, table_ref, brdf_ref, out_ref):
    rows = 8

    def some_rows(i, carry):
        here = pl.ds(pl.multiple_of(i * rows, rows), rows)
        for p in range(0, pixels, 128):
            at = (here, slice(p, p + 128))
            index, fraction = bin_ref[at], frac_ref[at]
            vol, geo = vol_ref[at], geo_ref[at]
            mask = mask_ref[at].astype(jnp.float32)
            for b in range(bands):
                line = jnp.broadcast_to(table_ref[b : b + 1, :], (rows, 128))
                lower = jnp.take_along_axis(line, index, axis=1)
                upper = jnp.take_along_axis(line, index + 1, axis=1)
                table_value = lower * (1.0 - fraction) + upper * fraction
                w0, w1, w2 = brdf_ref[b, 0], brdf_ref[b, 1], brdf_ref[b, 2]
                numerator = w0 + w1 * nadir_volume + w2 * nadir_geometric
                cfactor = numerator / (w0 + w1 * vol + w2 * geo)
                first = b * pixels + p
                out_ref[here, first : first + 128] = table_value * cfactor * mask
        return carry

    lax.fori_loop(0, out_ref.shape[0] // rows, some_rows, 0)


def finish_kernel(count, *refs):
    own_ref, parts = refs[0], refs[1 : 1 + count]
    low_ref, high_ref, factor_ref, out_ref = refs[1 + count :]
    grid = own_ref[...]
    for part in parts:
        grid = grid + part[...].astype(jnp.float32)
    before = jnp.concatenate([low_ref[...], grid[:-1]], axis=0)
    after = jnp.concatenate([grid[1:], high_ref[...]], axis=0)
    smoothed = 0.25 * before + 0.5 * grid + 0.25 * after
    out_ref[...] = (smoothed * factor_ref[...]).astype(jnp.bfloat16)


def on_device(
    swath_blocks,
    footprint,
    cell_row,
    tile_pick,
    sensor,
    bandpass_offset,
    weight_tiles,
    lookup_table,
    lookup_bin,
    lookup_frac,
    brdf_params,
    vol_kernel,
    geo_kernel,
    clear_mask,
):
    tiles, rows = lax.axis_size("tile"), lax.axis_size("row")
    devices = tiles * rows
    blocks, width = swath_blocks.shape[2], swath_blocks.shape[3]
    bands = bandpass_offset.shape[1]
    pixels = width // bands
    cells = lookup_bin.shape[1]
    capacity = max(2, 3 * blocks // (2 * devices))
    depth = tiles // 4
    peers = 2 * rows
    slots = depth * capacity
    bits = dict(z=4 * rows, x=2 * rows, core=rows, y=1)

    def exchange(array, flip):
        pairs = [(i, i ^ flip) for i in range(devices)]
        return lax.ppermute(array, ("tile", "row"), pairs)

    def chip_flip(k):
        return (k // rows) * bits["x"] + k % rows

    me = lax.axis_index("tile") * rows + lax.axis_index("row")
    relative = footprint.reshape(blocks) ^ me
    rel_z = relative // bits["z"]
    rel_x = relative // bits["x"] % 2
    rel_core = relative // bits["core"] % 2
    rel_y = relative % rows
    group = (rel_core * 2 + rel_x) * rows + rel_y
    key = rel_z * cells + cell_row.reshape(blocks)
    order = jnp.arange(blocks, dtype=jnp.int32)
    ahead = jnp.logical_and(group[:, None] == group[None, :], order[:, None] < order[None, :])
    position = group * slots + jnp.sum(ahead.astype(jnp.int32), axis=0)
    slot_ids = jnp.arange(2 * peers * slots, dtype=jnp.int32)
    tags = (
        jnp.sum(jnp.where(slot_ids[None, :] == position[:, None], key[:, None] + 1, 0), axis=0) - 1
    ).reshape(2, peers, slots)

    mixing = jnp.eye(bands, dtype=jnp.float32)[None] + bandpass_offset
    spread = (
        mixing[:, :, None, :, None] * jnp.eye(GROUP, dtype=jnp.float32)[None, None, :, None, :]
    ).reshape(2, bands * GROUP, bands * GROUP)
    high = lax.reduce_precision(spread, 8, 7)
    mix = jnp.stack([high, spread - high], axis=1)
    sensor_lanes = jnp.tile(sensor.reshape(blocks // GROUP, 1, GROUP), (1, 1, bands))

    resampled = pl.pallas_call(
        functools.partial(resample_kernel, bands, pixels),
        out_shape=jax.ShapeDtypeStruct((blocks, width), jnp.bfloat16),
        compiler_params=params(),
        name="resample",
    )(
        swath_blocks.reshape(blocks, width),
        sensor_lanes,
        tile_pick.reshape(blocks, 1),
        mix,
        weight_tiles,
    )

    other_tags = exchange(tags[1], bits["core"])
    tag_lists = []
    for k in range(peers):
        both = jnp.concatenate([tags[0, k], other_tags[k]])[None, :]
        tag_lists.append(both if k == 0 else exchange(both, chip_flip(k)))

    table = jnp.pad(lookup_table, ((0, 0), (0, 128 - lookup_table.shape[1])))
    vmem = pl.BlockSpec(memory_space=pltpu.VMEM)
    factor = pl.pallas_call(
        functools.partial(factor_kernel, bands, pixels),
        out_shape=jax.ShapeDtypeStruct((cells, width), jnp.float32),
        in_specs=[vmem] * 6 + [pl.BlockSpec(memory_space=pltpu.SMEM)],
        out_specs=vmem,
        compiler_params=params(),
        name="factor",
    )(lookup_bin[0], lookup_frac[0], vol_kernel[0], geo_kernel[0], clear_mask[0], table, brdf_params)

    results = []
    for begin, end in CHUNKS:
        first, last = begin * pixels, end * pixels
        columns = last - first
        own, other = pl.pallas_call(
            pack_kernel,
            out_shape=[jax.ShapeDtypeStruct((peers, slots, columns), jnp.bfloat16)] * 2,
            compiler_params=params(),
            name="pack",
        )(position.reshape(1, blocks), resampled[:, first:last])
        arrived = exchange(other, bits["core"])
        row_lists = []
        for k in range(peers):
            both = jnp.concatenate([own[k], arrived[k]], axis=0)
            row_lists.append(both if k == 0 else exchange(both, chip_flip(k)))
        mine, sends = pl.pallas_call(
            functools.partial(merge_kernel, peers, cells),
            out_shape=[
                jax.ShapeDtypeStruct((cells, columns), jnp.float32),
                jax.ShapeDtypeStruct((depth - 1, cells, columns), jnp.bfloat16),
            ],
            compiler_params=params(),
            name="merge",
        )(*tag_lists, *row_lists)
        parts = [exchange(sends[k - 1], k * bits["z"]) for k in range(1, depth)]
        first_row, last_row = mine[:1], mine[-1:]
        for part in parts:
            first_row = first_row + part[:1].astype(jnp.float32)
            last_row = last_row + part[-1:].astype(jnp.float32)
        up = [(i, i + 1) for i in range(rows - 1)]
        down = [(i + 1, i) for i in range(rows - 1)]
        low = lax.ppermute(last_row, "row", up)
        high_row = lax.ppermute(first_row, "row", down)
        result = pl.pallas_call(
            functools.partial(finish_kernel, depth - 1),
            out_shape=jax.ShapeDtypeStruct((cells, columns), jnp.bfloat16),
            compiler_params=params(),
            name="finish",
        )(mine, *parts, low, high_row, factor[:, first:last])
        results.append(result)
    return jnp.concatenate(results, axis=1).reshape(1, cells, width)


def solution(mesh):
    in_specs = (
        P("tile", "row", None, None),
        P("tile", "row", None, None),
        P("tile", "row", None),
        P("tile", "row", None),
        P("tile", "row", None),
        P(),
        P(),
        P(),
        P("tile", "row", None),
        P("tile", "row", None),
        P(),
        P("tile", "row", None),
        P("tile", "row", None),
        P("tile", "row", None),
    )
    out_specs = P("tile", "row", None)
    return jax.shard_map(
        on_device, mesh=mesh, in_specs=in_specs, out_specs=out_specs, check_vma=False
    )
```

```python
import functools

import jax
import jax.numpy as jnp
from jax import lax
from jax.experimental import pallas as pl
from jax.experimental.pallas import tpu as pltpu
from jax.sharding import PartitionSpec as P

nadir_volume = 0.3
nadir_geometric = 0.6

GROUP = 32
TAG_ROWS = 16
CHUNKS = ((0, 2), (2, 4), (4, 6), (6, 8))
ORDER = ("s0", "s1", "j0", "s2", "j1", "m0", "h0", "s3", "j2", "h0", "m1", "h1", "g0", "j3", "h1", "m2", "h2", "g1", "h2", "m3", "h3", "g2", "h3", "x0", "g3", "f0")
UNROLL = 6
SPLIT = (2, 1, 1)
MIB = 1024 * 1024


def call(kernel, name, limit, out_shape, operands, after, scalars=0, **more):
    vmem = pl.BlockSpec(memory_space=pltpu.VMEM)
    smem = pl.BlockSpec(memory_space=pltpu.SMEM)
    specs = more.pop("in_specs", None)
    if specs is None:
        specs = [smem] * scalars + [vmem] * (len(operands) - scalars)
    body = kernel
    if after is not None:
        specs = [pl.BlockSpec(memory_space=pl.ANY), *specs]
        operands = (after, *operands)

        def body(unused, *refs):
            kernel(*refs)

    return pl.pallas_call(
        body,
        out_shape=out_shape,
        in_specs=specs,
        out_specs=jax.tree.map(lambda _: vmem, out_shape),
        compiler_params=pltpu.CompilerParams(vmem_limit_bytes=limit * MIB),
        name=name,
        **more,
    )(*operands)


def dot(a, b):
    return jnp.dot(a, b, preferred_element_type=jnp.float32)


def one_hot(mask):
    return mask.astype(jnp.float32).astype(jnp.bfloat16)


def spread_mixing(offset_ref, s, b, bands):
    lane = lax.broadcasted_iota(jnp.int32, (GROUP, bands * GROUP), 1)
    row = lax.broadcasted_iota(jnp.int32, (GROUP, bands * GROUP), 0)
    total = jnp.zeros((GROUP, bands * GROUP), jnp.float32)
    for c in range(bands):
        value = offset_ref[s, b, c] + (1.0 if b == c else 0.0)
        total = jnp.where(lane == row + c * GROUP, value, total)
    return total


def routes(me, footprint, depth, rows):
    shift = rows.bit_length() - 1
    relative = jnp.bitwise_xor(footprint, me)
    rel_y = relative & (rows - 1)
    rel_core = lax.shift_right_logical(relative, shift) & 1
    rel_x = lax.shift_right_logical(relative, shift + 1) & 1
    rel_z = lax.shift_right_logical(relative, shift + 2)
    chip = rel_x * rows + rel_y
    if rows == 2:
        core = lax.shift_right_logical(me, shift) & 1
        swap = jnp.logical_and(core == 1, jnp.logical_or(chip == 1, chip == 2))
        chip = jnp.where(swap, 3 - chip, chip)
    return rel_z, chip * 2 + rel_core


def resample(shape, chunk, offset_ref, x_ref, wait, code_cols, weights_ref, banded_ref, result_ref):
    bands, pixels = shape[:2]
    begin, end = chunk
    blocks = x_ref.shape[0]
    count = end - begin
    tiles = weights_ref.shape[0]
    high, low = [], []
    for s in range(2):
        exact = jnp.concatenate(
            [spread_mixing(offset_ref, s, b, bands) for b in range(begin, end)], axis=0
        )
        upper = exact.astype(jnp.bfloat16)
        high.append(upper)
        low.append((exact - upper.astype(jnp.float32)).astype(jnp.bfloat16))
    mixers = jnp.concatenate(high + low, axis=0)
    size = count * GROUP

    def one_group(g):
        here = pl.ds(pl.multiple_of(g * GROUP, GROUP), GROUP)
        stacked = jnp.concatenate(
            [x_ref[here, c * pixels : (c + 1) * pixels] for c in range(bands)], axis=0
        )
        mixed = dot(mixers, stacked)
        first = mixed[:size] + mixed[2 * size : 3 * size]
        second = mixed[size : 2 * size] + mixed[3 * size :]
        lanes = code_cols[here, :]
        choice = jnp.concatenate([lanes] * (pixels // 128), axis=1) > tiles - 0.5
        for b in range(count):
            part = slice(b * GROUP, (b + 1) * GROUP)
            banded_ref[b, here, :] = jnp.where(choice, second[part], first[part]).astype(
                jnp.bfloat16
            )

    step = UNROLL * GROUP
    for start in range(0, blocks, step):
        wait(start, step)
        for g in range(start // GROUP, (start + step) // GROUP):
            one_group(g)

    code = jnp.concatenate([code_cols[...]] * (pixels // 128), axis=1)
    pick = jnp.where(code > tiles - 0.5, code - tiles, code)
    for b in range(count):
        banded = banded_ref[b].astype(jnp.float32)
        total = None
        for t in range(tiles):
            part = dot(jnp.where(pick == t, banded, 0.0).astype(jnp.bfloat16), weights_ref[t])
            total = part if total is None else total + part
        result_ref[:, b * pixels : (b + 1) * pixels] = total.astype(jnp.bfloat16)


def pack(position, slots, layout, result_ref, out_refs, tags=None):
    blocks = result_ref.shape[0]
    for chips, ref in zip(layout, out_refs):
        height = ref.shape[0] // len(chips)
        for i, k in enumerate(chips):
            ids = lax.broadcasted_iota(jnp.int32, (slots, blocks), 0) + k * slots
            chosen = one_hot(ids == position)
            start = i * height
            ref[start : start + slots, :] = dot(chosen, result_ref[...]).astype(jnp.bfloat16)
            if tags is not None:
                start, stop = start + slots, start + height
                ref[start:stop, :] = jnp.zeros((TAG_ROWS, ref.shape[1]), jnp.bfloat16)
                ref[start:stop, :slots] = lax.dot_general(
                    tags, chosen, (((1,), (1,)), ((), ())), preferred_element_type=jnp.float32
                ).astype(jnp.bfloat16)


def lead_kernel(shape, chunk, *refs):
    bands, pixels, rows, depth, slots, peers, layout = shape
    count = len(layout)
    ins, outs, scratch = refs[:8], refs[8 : 10 + count], refs[10 + count :]
    me_ref = ins[0]
    position_ref, code_cols = outs[count:]
    offset, x, foot, cell, pick, sensor, weights, banded_ref, result_ref, sems = scratch
    blocks = x.shape[0]
    tiles = weights.shape[0]
    step = UNROLL * GROUP
    small = [
        pltpu.make_async_copy(src, dst, sems.at[i])
        for i, (src, dst) in enumerate(
            ((ins[3], foot), (ins[4], cell), (ins[5], pick), (ins[6], sensor), (ins[1], offset))
        )
    ]
    matrices = pltpu.make_async_copy(ins[7], weights, sems.at[5])
    pieces = {
        start: pltpu.make_async_copy(
            ins[2].at[pl.ds(start, step), :], x.at[pl.ds(start, step), :], sems.at[6 + i]
        )
        for i, start in enumerate(range(0, blocks, step))
    }
    for copy in (*small, *pieces.values(), matrices):
        copy.start()
    for copy in small:
        copy.wait()

    code = pick[...] + tiles * sensor[...]
    code_cols[...] = jnp.broadcast_to(code.astype(jnp.float32), (128, blocks)).T

    place, group = routes(me_ref[0], foot[...], depth, rows)
    member = lax.broadcasted_iota(jnp.int32, (2 * peers, blocks), 0) == group
    member = member.astype(jnp.float32)
    earlier = lax.broadcasted_iota(jnp.int32, (blocks, blocks), 0) < lax.broadcasted_iota(
        jnp.int32, (blocks, blocks), 1
    )
    before = dot(member.astype(jnp.bfloat16), one_hot(earlier))
    rank = jnp.sum(member * before, axis=0, keepdims=True).astype(jnp.int32)
    position = group * (slots // 2) + rank
    position_ref[...] = position
    line = lax.broadcasted_iota(jnp.int32, (TAG_ROWS, blocks), 0)
    tags = jnp.where(line == 0, cell[...] + 1, jnp.where(line == 1, place, 0))
    tags = tags.astype(jnp.float32).astype(jnp.bfloat16)

    def wait(start, size):
        pieces[start].wait()
        if start == 0:
            matrices.wait()

    resample(shape, chunk, offset, x, wait, code_cols, weights, banded_ref, result_ref)
    pack(position, slots, layout, result_ref, outs[:count], tags)


def follow_kernel(shape, chunk, *refs):
    slots, layout = shape[4], shape[6]
    count = len(layout)
    offset_ref, x_ref, position_ref, code_cols, weights_ref = refs[:5]
    outs, (banded_ref, result_ref) = refs[5 : 5 + count], refs[5 + count :]
    resample(
        shape,
        chunk,
        offset_ref,
        x_ref,
        lambda start, size: None,
        code_cols,
        weights_ref,
        banded_ref,
        result_ref,
    )
    pack(position_ref[...], slots, layout, result_ref, outs)


def join_kernel(own_ref, arrived_ref, out_ref):
    height = own_ref.shape[0]
    out_ref[:height, :] = own_ref[...]
    out_ref[height:, :] = arrived_ref[height:, :]


def put(refs, planes):
    start = 0
    for ref in refs:
        ref[...] = planes[start : start + ref.shape[0]]
        start += ref.shape[0]


def merge_kernel(lead, slots, cells, parts, *refs):
    count = max(part[0] for part in parts) + 1
    rows = refs[:count]
    if lead:
        keep_ref, *sends, keys_ref = refs[count:]
    else:
        keys_ref, keep_ref, *sends = refs[count:]
    depth, columns = keep_ref.shape[0], keep_ref.shape[2]
    half = slots // 2
    ids = lax.broadcasted_iota(jnp.int32, (depth * cells, half), 0)
    for h in (1, 0):
        total = None
        for i, (j, start) in enumerate(parts):
            if lead:
                tag = rows[j][start + slots : start + slots + TAG_ROWS, h * half : (h + 1) * half]
                tag = tag.astype(jnp.float32)
                cell, place = tag[0:1].astype(jnp.int32), tag[1:2].astype(jnp.int32)
                key = place * cells + cell - 1
                keys_ref[2 * i + h] = key
            else:
                key = keys_ref[2 * i + h]
            first = start + h * half
            part = dot(one_hot(ids == key), rows[j][first : first + half, :])
            total = part if total is None else total + part
        total = total.reshape(depth, cells, columns)
        if h == 0:
            keep_ref[...] = total
        else:
            put(sends, total.astype(jnp.bfloat16))


def halve_kernel(count, *refs):
    kept_ref, arrived, keep_ref, sends = (
        refs[0],
        refs[1 : 1 + count],
        refs[1 + count],
        refs[2 + count :],
    )
    away = []
    start = 0
    for ref in arrived:
        for i in range(ref.shape[0]):
            plane = kept_ref[start] + ref[i].astype(jnp.float32)
            if start % 2 == 0:
                keep_ref[start // 2] = plane
            else:
                away.append(plane.astype(jnp.bfloat16)[None])
            start += 1
    put(sends, jnp.concatenate(away, axis=0))


def factor_kernel(bands, pixels, bin_ref, frac_ref, vol_ref, geo_ref, mask_ref, table_ref, brdf_ref, out_ref):
    rows = 8

    def some_rows(i, carry):
        here = pl.ds(pl.multiple_of(i * rows, rows), rows)
        for p in range(0, pixels, 128):
            at = (here, slice(p, p + 128))
            index, fraction = bin_ref[at], frac_ref[at]
            vol, geo = vol_ref[at], geo_ref[at]
            mask = mask_ref[at].astype(jnp.float32)
            for b in range(bands):
                line = jnp.broadcast_to(table_ref[b : b + 1, :], (rows, 128))
                lower = jnp.take_along_axis(line, index, axis=1)
                upper = jnp.take_along_axis(line, index + 1, axis=1)
                table_value = lower * (1.0 - fraction) + upper * fraction
                w0, w1, w2 = brdf_ref[b, 0], brdf_ref[b, 1], brdf_ref[b, 2]
                numerator = w0 + w1 * nadir_volume + w2 * nadir_geometric
                cfactor = numerator / (w0 + w1 * vol + w2 * geo)
                first = b * pixels + p
                out_ref[here, first : first + 128] = table_value * cfactor * mask
        return carry

    lax.fori_loop(0, out_ref.shape[0] // rows, some_rows, 0)


def total_kernel(kept_ref, arrived_ref, grid_ref):
    grid_ref[...] = kept_ref[0] + arrived_ref[0].astype(jnp.float32)


def finish_kernel(count, *refs):
    grids, (low_ref, high_ref, factor_ref, out_ref) = refs[:count], refs[count:]
    start = 0
    for grid_ref in grids:
        grid = grid_ref[...]
        here = slice(start, start + grid.shape[1])
        before = jnp.concatenate([low_ref[:, here], grid[:-1]], axis=0)
        after = jnp.concatenate([grid[1:], high_ref[:, here]], axis=0)
        smoothed = 0.25 * before + 0.5 * grid + 0.25 * after
        out_ref[:, here] = (smoothed * factor_ref[:, here]).astype(jnp.bfloat16)
        start = here.stop


def on_device(
    swath_blocks,
    footprint,
    cell_row,
    tile_pick,
    sensor,
    bandpass_offset,
    weight_tiles,
    lookup_table,
    lookup_bin,
    lookup_frac,
    brdf_params,
    vol_kernel,
    geo_kernel,
    clear_mask,
):
    tiles, rows = lax.axis_size("tile"), lax.axis_size("row")
    devices = tiles * rows
    blocks, width = swath_blocks.shape[2], swath_blocks.shape[3]
    bands = bandpass_offset.shape[1]
    pixels = width // bands
    cells = lookup_bin.shape[1]
    capacity = max(2, 3 * blocks // (2 * devices))
    depth = tiles // 4
    peers = 2 * rows
    slots = 2 * depth * capacity
    bits = dict(z=4 * rows, x=2 * rows, core=rows, y=1)

    def exchange(array, flip, other=None):
        flips = (flip, flip if other is None else other)
        pairs = [(i, i ^ flips[i // rows % 2]) for i in range(devices)]
        return lax.ppermute(array, ("tile", "row"), pairs)

    def chip_flip(k):
        return (k // rows) * bits["x"] + k % rows

    me = lax.axis_index("tile") * rows + lax.axis_index("row")
    smem = pl.BlockSpec(memory_space=pltpu.SMEM)
    hbm = pl.BlockSpec(memory_space=pltpu.HBM)
    layout = ((0,), (1, 3), (2,)) if rows == 2 else tuple((k,) for k in range(peers))
    shape = (bands, pixels, rows, depth, slots, peers, layout)
    x = swath_blocks.reshape(blocks, width)
    table = jnp.pad(lookup_table, ((0, 0), (0, 128 - lookup_table.shape[1])))
    flips = [bits["core"]] + [bits["z"] << i for i in range(depth.bit_length() - 1)]
    shared = {}
    chunks = [dict(hops=0) for _ in CHUNKS]

    def struct(*dims, dtype=jnp.bfloat16):
        return jax.ShapeDtypeStruct(dims, dtype)

    def send(i, after):
        begin, end = CHUNKS[i]
        columns = (end - begin) * pixels
        height = slots + (0 if i else TAG_ROWS)
        payload = [struct(len(chips) * height, columns) for chips in layout]
        work = [
            pltpu.VMEM((end - begin, blocks, pixels), jnp.bfloat16),
            pltpu.VMEM((blocks, columns), jnp.bfloat16),
        ]
        if i == 0:
            *lists, shared["position"], shared["codes"] = call(
                functools.partial(lead_kernel, shape, CHUNKS[i]),
                "lead",
                63,
                payload
                + [struct(1, blocks, dtype=jnp.int32), struct(blocks, 128, dtype=jnp.float32)],
                (
                    me.reshape(1).astype(jnp.int32),
                    bandpass_offset,
                    x,
                    footprint.reshape(1, blocks),
                    cell_row.reshape(1, blocks),
                    tile_pick.reshape(1, blocks),
                    sensor.reshape(1, blocks),
                    weight_tiles,
                ),
                after,
                in_specs=[smem] + [hbm] * 7,
                scratch_shapes=[
                    pltpu.SMEM(bandpass_offset.shape, jnp.float32),
                    pltpu.VMEM((blocks, width), jnp.bfloat16),
                    *[pltpu.VMEM((1, blocks), jnp.int32)] * 4,
                    pltpu.VMEM(weight_tiles.shape, jnp.bfloat16),
                    *work,
                    pltpu.SemaphoreType.DMA((6 + blocks // (UNROLL * GROUP),)),
                ],
            )
        else:
            lists = call(
                functools.partial(follow_kernel, shape, CHUNKS[i]),
                "follow",
                28,
                payload,
                (bandpass_offset, x, shared["position"], shared["codes"], weight_tiles),
                after,
                scalars=1,
                scratch_shapes=work,
            )
        if rows == 2:
            own, first, chunks[i]["second"] = lists
            chunks[i]["lists"] = [own, exchange(first, bits["y"], bits["x"])]
        else:
            chunks[i]["lists"] = [
                array if k == 0 else exchange(array, chip_flip(k)) for k, array in enumerate(lists)
            ]
        chunks[i]["parts"] = [(k, 0) for k in range(len(lists))]
        return lists[0]

    def join(i, after):
        if rows != 2:
            return after
        chunk = chunks[i]
        arrived = chunk["lists"][1]
        height, columns = arrived.shape
        both = call(
            join_kernel, "join", 16, struct(height, columns), (chunk["second"], arrived), after
        )
        chunk["lists"].append(exchange(both, bits["x"], bits["y"]))
        chunk["parts"] = [(0, 0), (1, 0), (2, 0), (2, height // 2)]
        return both

    def forward(i, keep, sends):
        chunk = chunks[i]
        chunk["keep"] = keep
        chunk["arrived"] = [exchange(array, flips[chunk["hops"]]) for array in sends]
        chunk["hops"] += 1
        return sends[0]

    def pieces(hop, planes, columns):
        count = min(planes, SPLIT[min(hop, 2)])
        return [struct(planes // count, cells, columns)] * count

    def merge(i, after):
        arrays = chunks[i]["lists"]
        columns = arrays[0].shape[1]
        parts = chunks[i]["parts"]
        outs = [struct(depth, cells, columns, dtype=jnp.float32), *pieces(0, depth, columns)]
        if i == 0:
            outs.append(struct(2 * peers, 1, slots // 2, dtype=jnp.int32))
        outs = call(
            functools.partial(merge_kernel, i == 0, slots, cells, parts),
            "merge",
            24,
            outs,
            (*arrays, *(() if i == 0 else (shared["keys"],))),
            after,
        )
        if i == 0:
            (*outs, shared["keys"]) = outs
        return forward(i, outs[0], outs[1:])

    def halve(i, after):
        keep, arrived = chunks[i]["keep"], chunks[i]["arrived"]
        half, columns = keep.shape[0] // 2, keep.shape[2]
        outs = call(
            functools.partial(halve_kernel, len(arrived)),
            "halve",
            16,
            [
                struct(half, cells, columns, dtype=jnp.float32),
                *pieces(chunks[i]["hops"], half, columns),
            ],
            (keep, *arrived),
            after,
        )
        return forward(i, outs[0], outs[1:])

    def total(i, after):
        chunk = chunks[i]
        while chunk["keep"].shape[0] > 1:
            after = halve(i, after)
        chunk["grid"] = call(
            total_kernel,
            "total",
            16,
            struct(*chunk["keep"].shape[1:], dtype=jnp.float32),
            (chunk["keep"], *chunk["arrived"]),
            after,
        )
        return chunk["grid"]

    def finish(i, after):
        first_row = jnp.concatenate([chunk["grid"][:1] for chunk in chunks], axis=1)
        last_row = jnp.concatenate([chunk["grid"][-1:] for chunk in chunks], axis=1)
        if rows == 2:
            upper_half = lax.axis_index("row") == 0
            edge = lax.ppermute(
                jnp.where(upper_half, last_row, first_row), "row", [(0, 1), (1, 0)]
            )
            low = jnp.where(upper_half, 0.0, edge)
            high = jnp.where(upper_half, edge, 0.0)
        else:
            low = lax.ppermute(last_row, "row", [(i, i + 1) for i in range(rows - 1)])
            high = lax.ppermute(first_row, "row", [(i + 1, i) for i in range(rows - 1)])
        return call(
            functools.partial(finish_kernel, len(chunks)),
            "finish",
            16,
            struct(cells, width),
            (
                *[chunk["grid"] for chunk in chunks],
                low,
                high,
                shared["factor"],
            ),
            after,
        )

    def factors(i, after):
        shared["factor"] = call(
            functools.partial(factor_kernel, bands, pixels),
            "factor",
            16,
            struct(cells, width, dtype=jnp.float32),
            (
                lookup_bin[0],
                lookup_frac[0],
                vol_kernel[0],
                geo_kernel[0],
                clear_mask[0],
                table,
                brdf_params,
            ),
            after,
            in_specs=[pl.BlockSpec(memory_space=pltpu.VMEM)] * 6 + [smem],
        )
        return shared["factor"]

    steps = dict(s=send, j=join, m=merge, h=halve, g=total, x=factors, f=finish)
    token = None
    for step in ORDER:
        token = steps[step[0]](int(step[1]), token)
    return token.reshape(1, cells, width)


def solution(mesh):
    in_specs = (
        P("tile", "row", None, None),
        P("tile", "row", None, None),
        P("tile", "row", None),
        P("tile", "row", None),
        P("tile", "row", None),
        P(),
        P(),
        P(),
        P("tile", "row", None),
        P("tile", "row", None),
        P(),
        P("tile", "row", None),
        P("tile", "row", None),
        P("tile", "row", None),
    )
    out_specs = P("tile", "row", None)
    return jax.shard_map(
        on_device, mesh=mesh, in_specs=in_specs, out_specs=out_specs, check_vma=False
    )
```

```python
import functools

import jax
import jax.numpy as jnp
from jax import lax
from jax.experimental import pallas as pl
from jax.experimental.pallas import tpu as pltpu
from jax.sharding import PartitionSpec as P

nadir_volume = 0.3
nadir_geometric = 0.6

GROUP = 32
TAG_ROWS = 16
CHUNKS = ((0, 2), (2, 4), (4, 6), (6, 8))
ORDER = (
    "s0",
    "k0",
    "s1",
    "k1",
    "j0",
    "s2",
    "s3",
    "k2",
    "j1",
    "m0",
    "h0",
    "k3",
    "j2",
    "m1",
    "h1",
    "g0",
    "j3",
    "m2",
    "g1",
    "h2",
    "m3",
    "g2",
    "h3",
    "x0",
    "f0",
)
UNROLL = 6
SPLIT = (1, 1)
MIB = 1024 * 1024


def call(kernel, name, limit, out_shape, operands, after, scalars=0, **more):
    vmem = pl.BlockSpec(memory_space=pltpu.VMEM)
    smem = pl.BlockSpec(memory_space=pltpu.SMEM)
    specs = more.pop("in_specs", None)
    if specs is None:
        specs = [smem] * scalars + [vmem] * (len(operands) - scalars)
    body = kernel
    if after is not None:
        specs = [pl.BlockSpec(memory_space=pl.ANY), *specs]
        operands = (after, *operands)

        def body(unused, *refs):
            kernel(*refs)

    return pl.pallas_call(
        body,
        out_shape=out_shape,
        in_specs=specs,
        out_specs=jax.tree.map(lambda _: vmem, out_shape),
        compiler_params=pltpu.CompilerParams(vmem_limit_bytes=limit * MIB),
        name=name,
        **more,
    )(*operands)


def dot(a, b):
    return jnp.dot(a, b, preferred_element_type=jnp.float32)


def one_hot(mask):
    return mask.astype(jnp.float32).astype(jnp.bfloat16)


def spread_mixing(offset_ref, s, b, bands):
    lane = lax.broadcasted_iota(jnp.int32, (GROUP, bands * GROUP), 1)
    row = lax.broadcasted_iota(jnp.int32, (GROUP, bands * GROUP), 0)
    total = jnp.zeros((GROUP, bands * GROUP), jnp.float32)
    for c in range(bands):
        value = offset_ref[s, b, c] + (1.0 if b == c else 0.0)
        total = jnp.where(lane == row + c * GROUP, value, total)
    return total


def routes(me, footprint, depth, rows):
    shift = rows.bit_length() - 1
    relative = jnp.bitwise_xor(footprint, me)
    rel_y = relative & (rows - 1)
    rel_core = lax.shift_right_logical(relative, shift) & 1
    rel_x = lax.shift_right_logical(relative, shift + 1) & 1
    rel_z = lax.shift_right_logical(relative, shift + 2)
    chip = rel_x * rows + rel_y
    if rows == 2:
        core = lax.shift_right_logical(footprint, shift) & 1
        swap = jnp.logical_and(core == 1, jnp.logical_or(chip == 1, chip == 2))
        chip = jnp.where(swap, 3 - chip, chip)
        chip = jnp.bitwise_xor(chip, lax.shift_right_logical(chip, 1))
    return rel_z, rel_core * 2 * rows + chip


def resample(shape, chunk, offset_ref, x_ref, wait, code_cols, weights_ref, banded_ref, result_ref):
    bands, pixels = shape[:2]
    begin, end = chunk
    blocks = x_ref.shape[0]
    count = end - begin
    tiles = weights_ref.shape[0]
    high, low = [], []
    for s in range(2):
        exact = jnp.concatenate(
            [spread_mixing(offset_ref, s, b, bands) for b in range(begin, end)], axis=0
        )
        upper = exact.astype(jnp.bfloat16)
        high.append(upper)
        low.append((exact - upper.astype(jnp.float32)).astype(jnp.bfloat16))
    mixers = jnp.concatenate(high + low, axis=0)
    size = count * GROUP

    def one_group(g):
        here = pl.ds(pl.multiple_of(g * GROUP, GROUP), GROUP)
        stacked = jnp.concatenate(
            [x_ref[here, c * pixels : (c + 1) * pixels] for c in range(bands)], axis=0
        )
        mixed = dot(mixers, stacked)
        first = mixed[:size] + mixed[2 * size : 3 * size]
        second = mixed[size : 2 * size] + mixed[3 * size :]
        lanes = code_cols[here, :]
        choice = jnp.concatenate([lanes] * (pixels // 128), axis=1) > tiles - 0.5
        for b in range(count):
            part = slice(b * GROUP, (b + 1) * GROUP)
            banded_ref[b, here, :] = jnp.where(choice, second[part], first[part]).astype(
                jnp.bfloat16
            )

    step = UNROLL * GROUP
    for start in range(0, blocks, step):
        wait(start, step)
        for g in range(start // GROUP, (start + step) // GROUP):
            one_group(g)

    code = jnp.concatenate([code_cols[...]] * (pixels // 128), axis=1)
    pick = jnp.where(code > tiles - 0.5, code - tiles, code)
    for b in range(count):
        banded = banded_ref[b].astype(jnp.float32)
        total = None
        for t in range(tiles):
            part = dot(jnp.where(pick == t, banded, 0.0).astype(jnp.bfloat16), weights_ref[t])
            total = part if total is None else total + part
        result_ref[:, b * pixels : (b + 1) * pixels] = total.astype(jnp.bfloat16)


def pack(position, slots, peers, result_ref, out_refs, tags=None):
    blocks = result_ref.shape[0]
    height = out_refs[0].shape[0] // peers
    for core, ref in enumerate(out_refs):
        for k in range(peers):
            ids = lax.broadcasted_iota(jnp.int32, (slots, blocks), 0) + (core * peers + k) * slots
            chosen = one_hot(ids == position)
            start = k * height
            ref[start : start + slots, :] = dot(chosen, result_ref[...]).astype(jnp.bfloat16)
            if tags is not None:
                start, stop = start + slots, start + height
                ref[start:stop, :] = jnp.zeros((TAG_ROWS, ref.shape[1]), jnp.bfloat16)
                ref[start:stop, :slots] = lax.dot_general(
                    tags, chosen, (((1,), (1,)), ((), ())), preferred_element_type=jnp.float32
                ).astype(jnp.bfloat16)


def lead_kernel(shape, chunk, *refs):
    bands, pixels, rows, depth, slots, peers = shape
    ins, outs, scratch = refs[:8], refs[8:12], refs[12:]
    me_ref = ins[0]
    position_ref, code_cols = outs[2:]
    offset, x, foot, cell, pick, sensor, weights, banded_ref, result_ref, sems = scratch
    blocks = x.shape[0]
    tiles = weights.shape[0]
    step = UNROLL * GROUP
    small = [
        pltpu.make_async_copy(src, dst, sems.at[i])
        for i, (src, dst) in enumerate(
            ((ins[3], foot), (ins[4], cell), (ins[5], pick), (ins[6], sensor), (ins[1], offset))
        )
    ]
    matrices = pltpu.make_async_copy(ins[7], weights, sems.at[5])
    pieces = {
        start: pltpu.make_async_copy(
            ins[2].at[pl.ds(start, step), :], x.at[pl.ds(start, step), :], sems.at[6 + i]
        )
        for i, start in enumerate(range(0, blocks, step))
    }
    for copy in (*small, *pieces.values(), matrices):
        copy.start()
    for copy in small:
        copy.wait()

    code = pick[...] + tiles * sensor[...]
    code_cols[...] = jnp.broadcast_to(code.astype(jnp.float32), (128, blocks)).T

    place, group = routes(me_ref[0], foot[...], depth, rows)
    member = lax.broadcasted_iota(jnp.int32, (2 * peers, blocks), 0) == group
    member = member.astype(jnp.float32)
    earlier = lax.broadcasted_iota(jnp.int32, (blocks, blocks), 0) < lax.broadcasted_iota(
        jnp.int32, (blocks, blocks), 1
    )
    before = dot(member.astype(jnp.bfloat16), one_hot(earlier))
    rank = jnp.sum(member * before, axis=0, keepdims=True).astype(jnp.int32)
    position = group * slots + rank
    position_ref[...] = position
    line = lax.broadcasted_iota(jnp.int32, (TAG_ROWS, blocks), 0)
    tags = jnp.where(line == 0, cell[...] + 1, jnp.where(line == 1, place, 0))
    tags = tags.astype(jnp.float32).astype(jnp.bfloat16)

    def wait(start, size):
        pieces[start].wait()
        if start == 0:
            matrices.wait()

    resample(shape, chunk, offset, x, wait, code_cols, weights, banded_ref, result_ref)
    pack(position, slots, peers, result_ref, outs[:2], tags)


def follow_kernel(shape, chunk, *refs):
    slots, peers = shape[4:]
    offset_ref, x_ref, position_ref, code_cols, weights_ref = refs[:5]
    outs, (banded_ref, result_ref) = refs[5:7], refs[7:]
    resample(
        shape,
        chunk,
        offset_ref,
        x_ref,
        lambda start, size: None,
        code_cols,
        weights_ref,
        banded_ref,
        result_ref,
    )
    pack(position_ref[...], slots, peers, result_ref, outs)


def fold_kernel(picks, peers, mine_ref, crossed_ref, *outs):
    height = mine_ref.shape[0] // peers
    for parts, ref in zip(picks, outs):
        start = 0
        for k in parts:
            for source in (mine_ref, crossed_ref):
                ref[start : start + height, :] = source[k * height : (k + 1) * height, :]
                start += height


def join_kernel(peers, mine_ref, crossed_ref, arrived_ref, out_ref):
    height = mine_ref.shape[0] // peers
    out_ref[:height, :] = mine_ref[-height:, :]
    out_ref[height : 2 * height, :] = crossed_ref[-height:, :]
    out_ref[2 * height :, :] = arrived_ref[2 * height :, :]


def put(refs, planes):
    start = 0
    for ref in refs:
        ref[...] = planes[start : start + ref.shape[0]]
        start += ref.shape[0]


def merge_kernel(lead, slots, cells, parts, *refs):
    count = max(part[0] for part in parts) + 1
    rows = refs[:count]
    if lead:
        keep_ref, *sends, keys_ref = refs[count:]
    else:
        keys_ref, keep_ref, *sends = refs[count:]
    depth, columns = 2 * keep_ref.shape[0], keep_ref.shape[2]
    ids = lax.broadcasted_iota(jnp.int32, (depth * cells, slots), 0)
    total = None
    for i, (j, start) in enumerate(parts):
        stop = start + slots
        if lead:
            tag = rows[j][stop : stop + TAG_ROWS, :slots].astype(jnp.float32)
            cell, place = tag[0:1].astype(jnp.int32), tag[1:2].astype(jnp.int32)
            key = place * cells + cell - 1
            keys_ref[i] = key
        else:
            key = keys_ref[i]
        part = dot(one_hot(ids == key), rows[j][start:stop, :])
        total = part if total is None else total + part
    total = total.reshape(depth // 2, 2, cells, columns)
    keep_ref[...] = total[:, 0]
    put(sends, total[:, 1].astype(jnp.bfloat16))


def halve_kernel(count, *refs):
    kept_ref, arrived, keep_ref, sends = (
        refs[0],
        refs[1 : 1 + count],
        refs[1 + count],
        refs[2 + count :],
    )
    away = []
    start = 0
    for ref in arrived:
        for i in range(ref.shape[0]):
            plane = kept_ref[start] + ref[i].astype(jnp.float32)
            if start % 2 == 0:
                keep_ref[start // 2] = plane
            else:
                away.append(plane.astype(jnp.bfloat16)[None])
            start += 1
    put(sends, jnp.concatenate(away, axis=0))


def factor_kernel(bands, pixels, bin_ref, frac_ref, vol_ref, geo_ref, mask_ref, table_ref, brdf_ref, out_ref):
    rows = 8

    def some_rows(i, carry):
        here = pl.ds(pl.multiple_of(i * rows, rows), rows)
        for p in range(0, pixels, 128):
            at = (here, slice(p, p + 128))
            index, fraction = bin_ref[at], frac_ref[at]
            vol, geo = vol_ref[at], geo_ref[at]
            mask = mask_ref[at].astype(jnp.float32)
            for b in range(bands):
                line = jnp.broadcast_to(table_ref[b : b + 1, :], (rows, 128))
                lower = jnp.take_along_axis(line, index, axis=1)
                upper = jnp.take_along_axis(line, index + 1, axis=1)
                table_value = lower * (1.0 - fraction) + upper * fraction
                w0, w1, w2 = brdf_ref[b, 0], brdf_ref[b, 1], brdf_ref[b, 2]
                numerator = w0 + w1 * nadir_volume + w2 * nadir_geometric
                cfactor = numerator / (w0 + w1 * vol + w2 * geo)
                first = b * pixels + p
                out_ref[here, first : first + 128] = table_value * cfactor * mask
        return carry

    lax.fori_loop(0, out_ref.shape[0] // rows, some_rows, 0)


def total_kernel(kept_ref, arrived_ref, grid_ref):
    grid_ref[...] = kept_ref[0] + arrived_ref[0].astype(jnp.float32)


def finish_kernel(count, *refs):
    grids, arrived_ref, (low_ref, high_ref, factor_ref, out_ref) = (
        refs[:count],
        refs[count],
        refs[count + 1 :],
    )
    start = 0
    for i, grid_ref in enumerate(grids):
        grid = grid_ref[...]
        if i == count - 1:
            grid = grid[0] + arrived_ref[...].astype(jnp.float32).reshape(grid.shape[1:])
        here = slice(start, start + grid.shape[1])
        before = jnp.concatenate([low_ref[:, here], grid[:-1]], axis=0)
        after = jnp.concatenate([grid[1:], high_ref[:, here]], axis=0)
        smoothed = 0.25 * before + 0.5 * grid + 0.25 * after
        out_ref[:, here] = (smoothed * factor_ref[:, here]).astype(jnp.bfloat16)
        start = here.stop


def on_device(
    swath_blocks,
    footprint,
    cell_row,
    tile_pick,
    sensor,
    bandpass_offset,
    weight_tiles,
    lookup_table,
    lookup_bin,
    lookup_frac,
    brdf_params,
    vol_kernel,
    geo_kernel,
    clear_mask,
):
    tiles, rows = lax.axis_size("tile"), lax.axis_size("row")
    devices = tiles * rows
    blocks, width = swath_blocks.shape[2], swath_blocks.shape[3]
    bands = bandpass_offset.shape[1]
    pixels = width // bands
    cells = lookup_bin.shape[1]
    capacity = max(2, 3 * blocks // (2 * devices))
    depth = tiles // 4
    peers = 2 * rows
    slots = depth * capacity
    bits = dict(z=4 * rows, x=2 * rows, core=rows, y=1)

    def exchange(array, flip, other=None):
        flips = (flip, flip if other is None else other)
        pairs = [(i, i ^ flips[i // rows % 2]) for i in range(devices)]
        return lax.ppermute(array, ("tile", "row"), pairs)

    def chip_flip(k):
        return (k // rows) * bits["x"] + k % rows

    me = lax.axis_index("tile") * rows + lax.axis_index("row")
    smem = pl.BlockSpec(memory_space=pltpu.SMEM)
    hbm = pl.BlockSpec(memory_space=pltpu.HBM)
    shape = (bands, pixels, rows, depth, slots, peers)
    x = swath_blocks.reshape(blocks, width)
    table = jnp.pad(lookup_table, ((0, 0), (0, 128 - lookup_table.shape[1])))
    picks = ((1, 2),) if rows == 2 else tuple((k,) for k in range(1, peers))
    shared = {}
    chunks = [dict(hops=0) for _ in CHUNKS]

    def struct(*dims, dtype=jnp.bfloat16):
        return jax.ShapeDtypeStruct(dims, dtype)

    def send(i, after):
        begin, end = CHUNKS[i]
        columns = (end - begin) * pixels
        height = slots + (0 if i else TAG_ROWS)
        payload = [struct(peers * height, columns)] * 2
        work = [
            pltpu.VMEM((end - begin, blocks, pixels), jnp.bfloat16),
            pltpu.VMEM((blocks, columns), jnp.bfloat16),
        ]
        if i == 0:
            mine, cross, shared["position"], shared["codes"] = call(
                functools.partial(lead_kernel, shape, CHUNKS[i]),
                "lead",
                63,
                payload
                + [struct(1, blocks, dtype=jnp.int32), struct(blocks, 128, dtype=jnp.float32)],
                (
                    me.reshape(1).astype(jnp.int32),
                    bandpass_offset,
                    x,
                    footprint.reshape(1, blocks),
                    cell_row.reshape(1, blocks),
                    tile_pick.reshape(1, blocks),
                    sensor.reshape(1, blocks),
                    weight_tiles,
                ),
                after,
                in_specs=[smem] + [hbm] * 7,
                scratch_shapes=[
                    pltpu.SMEM(bandpass_offset.shape, jnp.float32),
                    pltpu.VMEM((blocks, width), jnp.bfloat16),
                    *[pltpu.VMEM((1, blocks), jnp.int32)] * 4,
                    pltpu.VMEM(weight_tiles.shape, jnp.bfloat16),
                    *work,
                    pltpu.SemaphoreType.DMA((6 + blocks // (UNROLL * GROUP),)),
                ],
            )
        else:
            mine, cross = call(
                functools.partial(follow_kernel, shape, CHUNKS[i]),
                "follow",
                28,
                payload,
                (bandpass_offset, x, shared["position"], shared["codes"], weight_tiles),
                after,
                scalars=1,
                scratch_shapes=work,
            )
        chunks[i]["mine"], chunks[i]["crossed"] = mine, exchange(cross, bits["core"])
        return mine

    def fold(i, after):
        chunk = chunks[i]
        mine, crossed = chunk["mine"], chunk["crossed"]
        height, columns = mine.shape[0] // peers, mine.shape[1]
        outs = call(
            functools.partial(fold_kernel, picks, peers),
            "fold",
            16,
            [struct(2 * len(parts) * height, columns) for parts in picks],
            (mine, crossed),
            after,
        )
        if rows == 2:
            arrived = [exchange(outs[0], bits["y"], bits["x"])]
        else:
            arrived = [exchange(array, chip_flip(k + 1)) for k, array in enumerate(outs)]
        chunk["lists"] = [mine, crossed, *arrived]
        chunk["parts"] = [(0, 0), (1, 0)]
        for k in range(len(arrived)):
            chunk["parts"] += [(k + 2, 0), (k + 2, height)]
        return outs[0]

    def join(i, after):
        if rows != 2:
            return after
        chunk = chunks[i]
        arrived = chunk["lists"][2]
        both = call(
            functools.partial(join_kernel, peers),
            "join",
            16,
            struct(*arrived.shape),
            chunk["lists"],
            after,
        )
        chunk["lists"].append(exchange(both, bits["x"], bits["y"]))
        chunk["parts"] += [(3, k * (arrived.shape[0] // 4)) for k in range(4)]
        return both

    def forward(i, keep, sends):
        chunk = chunks[i]
        chunk["keep"] = keep
        chunk["away"] = sends[-1]
        chunk["arrived"] = [exchange(array, bits["z"] << chunk["hops"]) for array in sends]
        chunk["hops"] += 1
        return sends[0]

    def pieces(hop, planes, columns):
        count = min(planes, SPLIT[min(hop, 1)])
        return [struct(planes // count, cells, columns)] * count

    def merge(i, after):
        arrays = chunks[i]["lists"]
        columns = arrays[0].shape[1]
        parts = chunks[i]["parts"]
        outs = [struct(depth // 2, cells, columns, dtype=jnp.float32)]
        outs += pieces(0, depth // 2, columns)
        if i == 0:
            outs.append(struct(2 * peers, 1, slots, dtype=jnp.int32))
        outs = call(
            functools.partial(merge_kernel, i == 0, slots, cells, parts),
            "merge",
            24,
            outs,
            (*arrays, *(() if i == 0 else (shared["keys"],))),
            after,
        )
        if i == 0:
            (*outs, shared["keys"]) = outs
        return forward(i, outs[0], outs[1:])

    def halve(i, after):
        keep, arrived = chunks[i]["keep"], chunks[i]["arrived"]
        half, columns = keep.shape[0] // 2, keep.shape[2]
        outs = call(
            functools.partial(halve_kernel, len(arrived)),
            "halve",
            16,
            [
                struct(half, cells, columns, dtype=jnp.float32),
                *pieces(chunks[i]["hops"], half, columns),
            ],
            (keep, *arrived),
            after,
        )
        return forward(i, outs[0], outs[1:])

    def total(i, after):
        chunk = chunks[i]
        while chunk["keep"].shape[0] > 1:
            after = halve(i, after)
        chunk["grid"] = call(
            total_kernel,
            "total",
            16,
            struct(*chunk["keep"].shape[1:], dtype=jnp.float32),
            (chunk["keep"], *chunk["arrived"]),
            after,
        )
        return chunk["grid"]

    def finish(i, after):
        *early, final = chunks
        for i in range(len(chunks)):
            while chunks[i]["keep"].shape[0] > 1:
                after = halve(i, after)
            if i < len(early) and "grid" not in chunks[i]:
                after = total(i, after)
        keep, arrived = final["keep"], final["arrived"][0].reshape(cells, -1)
        away = final["away"].reshape(cells, -1)

        def ends(array):
            return array[:1], array[-1:]

        parts = []
        for pick in (0, 1):
            kept = [ends(chunk["grid"])[pick] for chunk in early] + [ends(keep[0])[pick]]
            parts.append((jnp.concatenate(kept, axis=1), ends(away)[pick]))
        width_early = width - arrived.shape[1]
        hop = bits["z"] << (final["hops"] - 1)

        def beside(kept, coming):
            coming = jnp.pad(coming.astype(jnp.float32), ((0, 0), (width_early, 0)))
            return kept + coming

        if rows == 2:
            upper = lax.axis_index("row") == 0
            kept = jnp.where(upper, parts[1][0], parts[0][0])
            coming = jnp.where(upper, parts[1][1], parts[0][1])
            row = beside(exchange(kept, 1), exchange(coming, hop ^ 1))
            low, high = jnp.where(upper, 0.0, row), jnp.where(upper, row, 0.0)
        else:
            up = [(i, i + 1) for i in range(rows - 1)]
            down = [(i + 1, i) for i in range(rows - 1)]
            across = [(t * rows + r, (t * rows + r) ^ hop) for t in range(tiles) for r in range(rows)]
            low_pairs = [(i, j + 1) for i, j in across if j % rows < rows - 1]
            high_pairs = [(i, j - 1) for i, j in across if j % rows > 0]
            axes = ("tile", "row")
            low = beside(
                lax.ppermute(parts[1][0], "row", up), lax.ppermute(parts[1][1], axes, low_pairs)
            )
            high = beside(
                lax.ppermute(parts[0][0], "row", down), lax.ppermute(parts[0][1], axes, high_pairs)
            )
        return call(
            functools.partial(finish_kernel, len(chunks)),
            "finish",
            16,
            struct(cells, width),
            (*[chunk["grid"] for chunk in early], keep, arrived, low, high, shared["factor"]),
            after,
        )

    def factors(i, after):
        shared["factor"] = call(
            functools.partial(factor_kernel, bands, pixels),
            "factor",
            16,
            struct(cells, width, dtype=jnp.float32),
            (
                lookup_bin[0],
                lookup_frac[0],
                vol_kernel[0],
                geo_kernel[0],
                clear_mask[0],
                table,
                brdf_params,
            ),
            after,
            in_specs=[pl.BlockSpec(memory_space=pltpu.VMEM)] * 6 + [smem],
        )
        return shared["factor"]

    steps = dict(s=send, k=fold, j=join, m=merge, h=halve, g=total, x=factors, f=finish)
    token = None
    for step in ORDER:
        token = steps[step[0]](int(step[1]), token)
    return token.reshape(1, cells, width)


def solution(mesh):
    in_specs = (
        P("tile", "row", None, None),
        P("tile", "row", None, None),
        P("tile", "row", None),
        P("tile", "row", None),
        P("tile", "row", None),
        P(),
        P(),
        P(),
        P("tile", "row", None),
        P("tile", "row", None),
        P(),
        P("tile", "row", None),
        P("tile", "row", None),
        P("tile", "row", None),
    )
    out_specs = P("tile", "row", None)
    return jax.shard_map(
        on_device, mesh=mesh, in_specs=in_specs, out_specs=out_specs, check_vma=False
    )
```

```python
import functools

import jax
import jax.numpy as jnp
from jax import lax
from jax.experimental import pallas as pl
from jax.experimental.pallas import tpu as pltpu
from jax.sharding import PartitionSpec as P

nadir_volume = 0.3
nadir_geometric = 0.6

GROUP = 32
TAG_ROWS = 16
CHUNKS = ((0, 2), (2, 4), (4, 6), (6, 8))
ORDER = (
    "s0",
    "k0",
    "s1",
    "k1",
    "j0",
    "s2",
    "s3",
    "k2",
    "j1",
    "m0",
    "h0",
    "k3",
    "j2",
    "m1",
    "h1",
    "g0",
    "j3",
    "m2",
    "g1",
    "h2",
    "m3",
    "g2",
    "h3",
    "x0",
    "g3",
    "f0",
)
UNROLL = 6
SPLIT = (1, 1)
MIB = 1024 * 1024


def call(kernel, name, weight, limit, out_shape, operands, after, scalars=0, **more):
    vmem = pl.BlockSpec(memory_space=pltpu.VMEM)
    smem = pl.BlockSpec(memory_space=pltpu.SMEM)
    specs = more.pop("in_specs", None)
    if specs is None:
        specs = [smem] * scalars + [vmem] * (len(operands) - scalars)
    body = kernel
    if after is not None:
        specs = [pl.BlockSpec(memory_space=pl.ANY), *specs]
        operands = (after, *operands)

        def body(unused, *refs):
            kernel(*refs)

    return pl.pallas_call(
        body,
        out_shape=out_shape,
        in_specs=specs,
        out_specs=jax.tree.map(lambda _: vmem, out_shape),
        compiler_params=pltpu.CompilerParams(vmem_limit_bytes=limit * MIB),
        cost_estimate=cost(weight),
        name=name,
        **more,
    )(*operands)


def cost(weight):
    return pl.CostEstimate(
        flops=int(weight * 1.1e6), bytes_accessed=int(weight * 3.6e3), transcendentals=0
    )


def dot(a, b):
    return jnp.dot(a, b, preferred_element_type=jnp.float32)


def one_hot(mask):
    return mask.astype(jnp.float32).astype(jnp.bfloat16)


def spread_mixing(offset_ref, s, b, bands):
    lane = lax.broadcasted_iota(jnp.int32, (GROUP, bands * GROUP), 1)
    row = lax.broadcasted_iota(jnp.int32, (GROUP, bands * GROUP), 0)
    total = jnp.zeros((GROUP, bands * GROUP), jnp.float32)
    for c in range(bands):
        value = offset_ref[s, b, c] + (1.0 if b == c else 0.0)
        total = jnp.where(lane == row + c * GROUP, value, total)
    return total


def routes(me, footprint, depth, rows):
    shift = rows.bit_length() - 1
    relative = jnp.bitwise_xor(footprint, me)
    rel_y = relative & (rows - 1)
    rel_core = lax.shift_right_logical(relative, shift) & 1
    rel_x = lax.shift_right_logical(relative, shift + 1) & 1
    rel_z = lax.shift_right_logical(relative, shift + 2)
    chip = rel_x * rows + rel_y
    if rows == 2:
        core = lax.shift_right_logical(footprint, shift) & 1
        swap = jnp.logical_and(core == 1, jnp.logical_or(chip == 1, chip == 2))
        chip = jnp.where(swap, 3 - chip, chip)
        chip = jnp.bitwise_xor(chip, lax.shift_right_logical(chip, 1))
    return rel_z, rel_core * 2 * rows + chip


def resample(shape, chunk, offset_ref, x_ref, wait, code_cols, weights_ref, banded_ref, result_ref):
    bands, pixels = shape[:2]
    begin, end = chunk
    blocks = x_ref.shape[0]
    count = end - begin
    tiles = weights_ref.shape[0]
    high, low = [], []
    for s in range(2):
        exact = jnp.concatenate(
            [spread_mixing(offset_ref, s, b, bands) for b in range(begin, end)], axis=0
        )
        upper = exact.astype(jnp.bfloat16)
        high.append(upper)
        low.append((exact - upper.astype(jnp.float32)).astype(jnp.bfloat16))
    mixers = jnp.concatenate(high + low, axis=0)
    size = count * GROUP

    def one_group(g):
        here = pl.ds(pl.multiple_of(g * GROUP, GROUP), GROUP)
        stacked = jnp.concatenate(
            [x_ref[here, c * pixels : (c + 1) * pixels] for c in range(bands)], axis=0
        )
        mixed = dot(mixers, stacked)
        first = mixed[:size] + mixed[2 * size : 3 * size]
        second = mixed[size : 2 * size] + mixed[3 * size :]
        lanes = code_cols[here, :]
        choice = jnp.concatenate([lanes] * (pixels // 128), axis=1) > tiles - 0.5
        for b in range(count):
            part = slice(b * GROUP, (b + 1) * GROUP)
            banded_ref[b, here, :] = jnp.where(choice, second[part], first[part]).astype(
                jnp.bfloat16
            )

    step = UNROLL * GROUP
    for start in range(0, blocks, step):
        wait(start, step)
        for g in range(start // GROUP, (start + step) // GROUP):
            one_group(g)

    code = jnp.concatenate([code_cols[...]] * (pixels // 128), axis=1)
    pick = jnp.where(code > tiles - 0.5, code - tiles, code)
    for b in range(count):
        banded = banded_ref[b].astype(jnp.float32)
        total = None
        for t in range(tiles):
            part = dot(jnp.where(pick == t, banded, 0.0).astype(jnp.bfloat16), weights_ref[t])
            total = part if total is None else total + part
        result_ref[:, b * pixels : (b + 1) * pixels] = total.astype(jnp.bfloat16)


def pack(position, slots, peers, result_ref, out_refs, tags=None):
    blocks = result_ref.shape[0]
    height = out_refs[0].shape[0] // peers
    for core, ref in enumerate(out_refs):
        for k in range(peers):
            ids = lax.broadcasted_iota(jnp.int32, (slots, blocks), 0) + (core * peers + k) * slots
            chosen = one_hot(ids == position)
            start = k * height
            ref[start : start + slots, :] = dot(chosen, result_ref[...]).astype(jnp.bfloat16)
            if tags is not None:
                start, stop = start + slots, start + height
                ref[start:stop, :] = jnp.zeros((TAG_ROWS, ref.shape[1]), jnp.bfloat16)
                ref[start:stop, :slots] = lax.dot_general(
                    tags, chosen, (((1,), (1,)), ((), ())), preferred_element_type=jnp.float32
                ).astype(jnp.bfloat16)


def lead_kernel(shape, chunk, *refs):
    bands, pixels, rows, depth, slots, peers = shape
    ins, outs, scratch = refs[:8], refs[8:12], refs[12:]
    me_ref = ins[0]
    position_ref, code_cols = outs[2:]
    offset, x, foot, cell, pick, sensor, weights, banded_ref, result_ref, sems = scratch
    blocks = x.shape[0]
    tiles = weights.shape[0]
    step = UNROLL * GROUP
    small = [
        pltpu.make_async_copy(src, dst, sems.at[i])
        for i, (src, dst) in enumerate(
            ((ins[3], foot), (ins[4], cell), (ins[5], pick), (ins[6], sensor), (ins[1], offset))
        )
    ]
    matrices = pltpu.make_async_copy(ins[7], weights, sems.at[5])
    pieces = {
        start: pltpu.make_async_copy(
            ins[2].at[pl.ds(start, step), :], x.at[pl.ds(start, step), :], sems.at[6 + i]
        )
        for i, start in enumerate(range(0, blocks, step))
    }
    for copy in (*small, *pieces.values(), matrices):
        copy.start()
    for copy in small:
        copy.wait()

    code = pick[...] + tiles * sensor[...]
    code_cols[...] = jnp.broadcast_to(code.astype(jnp.float32), (128, blocks)).T

    place, group = routes(me_ref[0], foot[...], depth, rows)
    member = lax.broadcasted_iota(jnp.int32, (2 * peers, blocks), 0) == group
    member = member.astype(jnp.float32)
    earlier = lax.broadcasted_iota(jnp.int32, (blocks, blocks), 0) < lax.broadcasted_iota(
        jnp.int32, (blocks, blocks), 1
    )
    before = dot(member.astype(jnp.bfloat16), one_hot(earlier))
    rank = jnp.sum(member * before, axis=0, keepdims=True).astype(jnp.int32)
    position = group * slots + rank
    position_ref[...] = position
    line = lax.broadcasted_iota(jnp.int32, (TAG_ROWS, blocks), 0)
    tags = jnp.where(line == 0, cell[...] + 1, jnp.where(line == 1, place, 0))
    tags = tags.astype(jnp.float32).astype(jnp.bfloat16)

    def wait(start, size):
        pieces[start].wait()
        if start == 0:
            matrices.wait()

    resample(shape, chunk, offset, x, wait, code_cols, weights, banded_ref, result_ref)
    pack(position, slots, peers, result_ref, outs[:2], tags)


def follow_kernel(shape, chunk, *refs):
    slots, peers = shape[4:]
    offset_ref, x_ref, position_ref, code_cols, weights_ref = refs[:5]
    outs, (banded_ref, result_ref) = refs[5:7], refs[7:]
    resample(
        shape,
        chunk,
        offset_ref,
        x_ref,
        lambda start, size: None,
        code_cols,
        weights_ref,
        banded_ref,
        result_ref,
    )
    pack(position_ref[...], slots, peers, result_ref, outs)


def fold_kernel(picks, peers, mine_ref, crossed_ref, *outs):
    height = mine_ref.shape[0] // peers
    for parts, ref in zip(picks, outs):
        start = 0
        for k in parts:
            for source in (mine_ref, crossed_ref):
                ref[start : start + height, :] = source[k * height : (k + 1) * height, :]
                start += height


def join_kernel(peers, mine_ref, crossed_ref, arrived_ref, out_ref):
    height = mine_ref.shape[0] // peers
    out_ref[:height, :] = mine_ref[-height:, :]
    out_ref[height : 2 * height, :] = crossed_ref[-height:, :]
    out_ref[2 * height :, :] = arrived_ref[2 * height :, :]


def put(refs, planes):
    start = 0
    for ref in refs:
        ref[...] = planes[start : start + ref.shape[0]]
        start += ref.shape[0]


def merge_kernel(lead, slots, cells, parts, *refs):
    count = max(part[0] for part in parts) + 1
    rows = refs[:count]
    if lead:
        keep_ref, *sends, keys_ref = refs[count:]
    else:
        keys_ref, keep_ref, *sends = refs[count:]
    depth, columns = 2 * keep_ref.shape[0], keep_ref.shape[2]
    ids = lax.broadcasted_iota(jnp.int32, (depth * cells, slots), 0)
    total = None
    for i, (j, start) in enumerate(parts):
        stop = start + slots
        if lead:
            tag = rows[j][stop : stop + TAG_ROWS, :slots].astype(jnp.float32)
            cell, place = tag[0:1].astype(jnp.int32), tag[1:2].astype(jnp.int32)
            key = place * cells + cell - 1
            keys_ref[i] = key
        else:
            key = keys_ref[i]
        part = dot(one_hot(ids == key), rows[j][start:stop, :])
        total = part if total is None else total + part
    total = total.reshape(depth // 2, 2, cells, columns)
    keep_ref[...] = total[:, 0]
    put(sends, total[:, 1].astype(jnp.bfloat16))


def halve_kernel(count, *refs):
    kept_ref, arrived, keep_ref, sends = (
        refs[0],
        refs[1 : 1 + count],
        refs[1 + count],
        refs[2 + count :],
    )
    away = []
    start = 0
    for ref in arrived:
        for i in range(ref.shape[0]):
            plane = kept_ref[start] + ref[i].astype(jnp.float32)
            if start % 2 == 0:
                keep_ref[start // 2] = plane
            else:
                away.append(plane.astype(jnp.bfloat16)[None])
            start += 1
    put(sends, jnp.concatenate(away, axis=0))


def factor_kernel(bands, pixels, bin_ref, frac_ref, vol_ref, geo_ref, mask_ref, table_ref, brdf_ref, out_ref):
    rows = 8

    def some_rows(i, carry):
        here = pl.ds(pl.multiple_of(i * rows, rows), rows)
        for p in range(0, pixels, 128):
            at = (here, slice(p, p + 128))
            index, fraction = bin_ref[at], frac_ref[at]
            vol, geo = vol_ref[at], geo_ref[at]
            mask = mask_ref[at].astype(jnp.float32)
            for b in range(bands):
                line = jnp.broadcast_to(table_ref[b : b + 1, :], (rows, 128))
                lower = jnp.take_along_axis(line, index, axis=1)
                upper = jnp.take_along_axis(line, index + 1, axis=1)
                table_value = lower * (1.0 - fraction) + upper * fraction
                w0, w1, w2 = brdf_ref[b, 0], brdf_ref[b, 1], brdf_ref[b, 2]
                numerator = w0 + w1 * nadir_volume + w2 * nadir_geometric
                cfactor = numerator / (w0 + w1 * vol + w2 * geo)
                first = b * pixels + p
                out_ref[here, first : first + 128] = table_value * cfactor * mask
        return carry

    lax.fori_loop(0, out_ref.shape[0] // rows, some_rows, 0)


def total_kernel(kept_ref, arrived_ref, grid_ref):
    grid_ref[...] = kept_ref[0] + arrived_ref[0].astype(jnp.float32)


def finish_kernel(count, *refs):
    grids, (low_ref, high_ref, factor_ref, out_ref) = refs[:count], refs[count:]
    start = 0
    for grid_ref in grids:
        grid = grid_ref[...]
        here = slice(start, start + grid.shape[1])
        before = jnp.concatenate([low_ref[:, here], grid[:-1]], axis=0)
        after = jnp.concatenate([grid[1:], high_ref[:, here]], axis=0)
        smoothed = 0.25 * before + 0.5 * grid + 0.25 * after
        out_ref[:, here] = (smoothed * factor_ref[:, here]).astype(jnp.bfloat16)
        start = here.stop


def on_device(
    swath_blocks,
    footprint,
    cell_row,
    tile_pick,
    sensor,
    bandpass_offset,
    weight_tiles,
    lookup_table,
    lookup_bin,
    lookup_frac,
    brdf_params,
    vol_kernel,
    geo_kernel,
    clear_mask,
):
    tiles, rows = lax.axis_size("tile"), lax.axis_size("row")
    devices = tiles * rows
    blocks, width = swath_blocks.shape[2], swath_blocks.shape[3]
    bands = bandpass_offset.shape[1]
    pixels = width // bands
    cells = lookup_bin.shape[1]
    capacity = max(2, 3 * blocks // (2 * devices))
    depth = tiles // 4
    peers = 2 * rows
    slots = depth * capacity
    bits = dict(z=4 * rows, x=2 * rows, core=rows, y=1)

    def exchange(array, flip, other=None):
        flips = (flip, flip if other is None else other)
        pairs = [(i, i ^ flips[i // rows % 2]) for i in range(devices)]
        return lax.ppermute(array, ("tile", "row"), pairs)

    def chip_flip(k):
        return (k // rows) * bits["x"] + k % rows

    me = lax.axis_index("tile") * rows + lax.axis_index("row")
    smem = pl.BlockSpec(memory_space=pltpu.SMEM)
    hbm = pl.BlockSpec(memory_space=pltpu.HBM)
    shape = (bands, pixels, rows, depth, slots, peers)
    x = swath_blocks.reshape(blocks, width)
    table = jnp.pad(lookup_table, ((0, 0), (0, 128 - lookup_table.shape[1])))
    picks = ((1, 2),) if rows == 2 else tuple((k,) for k in range(1, peers))
    shared = {}
    chunks = [dict(hops=0) for _ in CHUNKS]

    def struct(*dims, dtype=jnp.bfloat16):
        return jax.ShapeDtypeStruct(dims, dtype)

    def send(i, after):
        begin, end = CHUNKS[i]
        columns = (end - begin) * pixels
        height = slots + (0 if i else TAG_ROWS)
        payload = [struct(peers * height, columns)] * 2
        work = [
            pltpu.VMEM((end - begin, blocks, pixels), jnp.bfloat16),
            pltpu.VMEM((blocks, columns), jnp.bfloat16),
        ]
        if i == 0:
            mine, cross, shared["position"], shared["codes"] = call(
                functools.partial(lead_kernel, shape, CHUNKS[i]),
                "lead",
                6,
                63,
                payload
                + [struct(1, blocks, dtype=jnp.int32), struct(blocks, 128, dtype=jnp.float32)],
                (
                    me.reshape(1).astype(jnp.int32),
                    bandpass_offset,
                    x,
                    footprint.reshape(1, blocks),
                    cell_row.reshape(1, blocks),
                    tile_pick.reshape(1, blocks),
                    sensor.reshape(1, blocks),
                    weight_tiles,
                ),
                after,
                in_specs=[smem] + [hbm] * 7,
                scratch_shapes=[
                    pltpu.SMEM(bandpass_offset.shape, jnp.float32),
                    pltpu.VMEM((blocks, width), jnp.bfloat16),
                    *[pltpu.VMEM((1, blocks), jnp.int32)] * 4,
                    pltpu.VMEM(weight_tiles.shape, jnp.bfloat16),
                    *work,
                    pltpu.SemaphoreType.DMA((6 + blocks // (UNROLL * GROUP),)),
                ],
            )
        else:
            mine, cross = call(
                functools.partial(follow_kernel, shape, CHUNKS[i]),
                "follow",
                2 + (end - begin),
                28,
                payload,
                (bandpass_offset, x, shared["position"], shared["codes"], weight_tiles),
                after,
                scalars=1,
                scratch_shapes=work,
            )
        chunks[i]["mine"], chunks[i]["crossed"] = mine, exchange(cross, bits["core"])
        return mine

    def fold(i, after):
        chunk = chunks[i]
        mine, crossed = chunk["mine"], chunk["crossed"]
        height, columns = mine.shape[0] // peers, mine.shape[1]
        outs = call(
            functools.partial(fold_kernel, picks, peers),
            "fold",
            0.3,
            16,
            [struct(2 * len(parts) * height, columns) for parts in picks],
            (mine, crossed),
            after,
        )
        if rows == 2:
            arrived = [exchange(outs[0], bits["y"], bits["x"])]
        else:
            arrived = [exchange(array, chip_flip(k + 1)) for k, array in enumerate(outs)]
        chunk["lists"] = [mine, crossed, *arrived]
        chunk["parts"] = [(0, 0), (1, 0)]
        for k in range(len(arrived)):
            chunk["parts"] += [(k + 2, 0), (k + 2, height)]
        return outs[0]

    def join(i, after):
        if rows != 2:
            return after
        chunk = chunks[i]
        arrived = chunk["lists"][2]
        both = call(
            functools.partial(join_kernel, peers),
            "join",
            0.3,
            16,
            struct(*arrived.shape),
            chunk["lists"],
            after,
        )
        chunk["lists"].append(exchange(both, bits["x"], bits["y"]))
        chunk["parts"] += [(3, k * (arrived.shape[0] // 4)) for k in range(4)]
        return both

    def forward(i, keep, sends):
        chunk = chunks[i]
        chunk["keep"] = keep
        chunk["away"] = sends[-1]
        chunk["arrived"] = [exchange(array, bits["z"] << chunk["hops"]) for array in sends]
        chunk["hops"] += 1
        return sends[0]

    def pieces(hop, planes, columns):
        count = min(planes, SPLIT[min(hop, 1)])
        return [struct(planes // count, cells, columns)] * count

    def merge(i, after):
        arrays = chunks[i]["lists"]
        columns = arrays[0].shape[1]
        parts = chunks[i]["parts"]
        outs = [struct(depth // 2, cells, columns, dtype=jnp.float32)]
        outs += pieces(0, depth // 2, columns)
        if i == 0:
            outs.append(struct(2 * peers, 1, slots, dtype=jnp.int32))
        outs = call(
            functools.partial(merge_kernel, i == 0, slots, cells, parts),
            "merge",
            0.5 + 0.7 * columns / pixels,
            24,
            outs,
            (*arrays, *(() if i == 0 else (shared["keys"],))),
            after,
        )
        if i == 0:
            (*outs, shared["keys"]) = outs
        return forward(i, outs[0], outs[1:])

    def halve(i, after):
        keep, arrived = chunks[i]["keep"], chunks[i]["arrived"]
        half, columns = keep.shape[0] // 2, keep.shape[2]
        outs = call(
            functools.partial(halve_kernel, len(arrived)),
            "halve",
            0.5,
            16,
            [
                struct(half, cells, columns, dtype=jnp.float32),
                *pieces(chunks[i]["hops"], half, columns),
            ],
            (keep, *arrived),
            after,
        )
        if i == len(chunks) - 1 and half == 1:
            chunks[i]["edges"] = edges(outs[0], outs[-1].reshape(cells, -1))
        return forward(i, outs[0], outs[1:])

    def total(i, after):
        chunk = chunks[i]
        while chunk["keep"].shape[0] > 1:
            after = halve(i, after)
        chunk["grid"] = call(
            total_kernel,
            "total",
            0.3,
            16,
            struct(*chunk["keep"].shape[1:], dtype=jnp.float32),
            (chunk["keep"], *chunk["arrived"]),
            after,
        )
        return chunk["grid"]

    def edges(keep, away):
        early = chunks[:-1]
        def ends(array):
            return array[:1], array[-1:]

        parts = []
        for pick in (0, 1):
            kept = [ends(chunk["grid"])[pick] for chunk in early] + [ends(keep[0])[pick]]
            parts.append((jnp.concatenate(kept, axis=1), ends(away)[pick]))
        width_early = width - away.shape[1]
        hop = bits["z"] << (depth.bit_length() - 2)

        def beside(kept, coming):
            coming = jnp.pad(coming.astype(jnp.float32), ((0, 0), (width_early, 0)))
            return kept + coming

        if rows == 2:
            upper = lax.axis_index("row") == 0
            kept = jnp.where(upper, parts[1][0], parts[0][0])
            coming = jnp.where(upper, parts[1][1], parts[0][1])
            row = beside(exchange(kept, 1), exchange(coming, hop ^ 1))
            low, high = jnp.where(upper, 0.0, row), jnp.where(upper, row, 0.0)
        else:
            up = [(i, i + 1) for i in range(rows - 1)]
            down = [(i + 1, i) for i in range(rows - 1)]
            across = [(t * rows + r, (t * rows + r) ^ hop) for t in range(tiles) for r in range(rows)]
            low_pairs = [(i, j + 1) for i, j in across if j % rows < rows - 1]
            high_pairs = [(i, j - 1) for i, j in across if j % rows > 0]
            axes = ("tile", "row")
            low = beside(
                lax.ppermute(parts[1][0], "row", up), lax.ppermute(parts[1][1], axes, low_pairs)
            )
            high = beside(
                lax.ppermute(parts[0][0], "row", down), lax.ppermute(parts[0][1], axes, high_pairs)
            )
        return low, high

    def finish(i, after):
        low, high = chunks[-1]["edges"]
        return call(
            functools.partial(finish_kernel, len(chunks)),
            "finish",
            1,
            16,
            struct(cells, width),
            (*[chunk["grid"] for chunk in chunks], low, high, shared["factor"]),
            after,
        )

    def factors(i, after):
        shared["factor"] = call(
            functools.partial(factor_kernel, bands, pixels),
            "factor",
            3,
            16,
            struct(cells, width, dtype=jnp.float32),
            (
                lookup_bin[0],
                lookup_frac[0],
                vol_kernel[0],
                geo_kernel[0],
                clear_mask[0],
                table,
                brdf_params,
            ),
            after,
            in_specs=[pl.BlockSpec(memory_space=pltpu.VMEM)] * 6 + [smem],
        )
        return shared["factor"]

    steps = dict(s=send, k=fold, j=join, m=merge, h=halve, g=total, x=factors, f=finish)
    token = None
    for step in ORDER:
        token = steps[step[0]](int(step[1]), token)
    return token.reshape(1, cells, width)


def solution(mesh):
    in_specs = (
        P("tile", "row", None, None),
        P("tile", "row", None, None),
        P("tile", "row", None),
        P("tile", "row", None),
        P("tile", "row", None),
        P(),
        P(),
        P(),
        P("tile", "row", None),
        P("tile", "row", None),
        P(),
        P("tile", "row", None),
        P("tile", "row", None),
        P("tile", "row", None),
    )
    out_specs = P("tile", "row", None)
    return jax.shard_map(
        on_device, mesh=mesh, in_specs=in_specs, out_specs=out_specs, check_vma=False
    )
```

```python
import functools

import jax
import jax.numpy as jnp
from jax import lax
from jax.experimental import pallas as pl
from jax.experimental.pallas import tpu as pltpu
from jax.sharding import PartitionSpec as P

nadir_volume = 0.3
nadir_geometric = 0.6

GROUP = 32
TAG_ROWS = 16
CHUNKS = ((0, 2), (2, 4), (4, 6), (6, 8))
ORDER = (
    "s0",
    "k0",
    "s1",
    "k1",
    "j0",
    "s2",
    "s3",
    "k2",
    "j1",
    "m0",
    "h0",
    "k3",
    "j2",
    "m1",
    "h1",
    "g0",
    "j3",
    "m2",
    "m3",
    "g1",
    "h2",
    "g2",
    "h3",
    "x0",
    "g3",
    "f0",
)
UNROLL = 6
SPLIT = (1, 1)
MIB = 1024 * 1024


def call(kernel, name, weight, limit, out_shape, operands, after, scalars=0, **more):
    vmem = pl.BlockSpec(memory_space=pltpu.VMEM)
    smem = pl.BlockSpec(memory_space=pltpu.SMEM)
    specs = more.pop("in_specs", None)
    if specs is None:
        specs = [smem] * scalars + [vmem] * (len(operands) - scalars)
    body = kernel
    if after is not None:
        specs = [pl.BlockSpec(memory_space=pl.ANY), *specs]
        operands = (after, *operands)

        def body(unused, *refs):
            kernel(*refs)

    return pl.pallas_call(
        body,
        out_shape=out_shape,
        in_specs=specs,
        out_specs=jax.tree.map(lambda _: vmem, out_shape),
        compiler_params=pltpu.CompilerParams(vmem_limit_bytes=limit * MIB),
        cost_estimate=cost(weight),
        name=name,
        **more,
    )(*operands)


def cost(weight):
    return pl.CostEstimate(
        flops=int(weight * 1.1e6), bytes_accessed=int(weight * 3.6e3), transcendentals=0
    )


def dot(a, b):
    return jnp.dot(a, b, preferred_element_type=jnp.float32)


def one_hot(mask):
    return mask.astype(jnp.float32).astype(jnp.bfloat16)


def spread_mixing(offset_ref, s, b, bands):
    lane = lax.broadcasted_iota(jnp.int32, (GROUP, bands * GROUP), 1)
    row = lax.broadcasted_iota(jnp.int32, (GROUP, bands * GROUP), 0)
    total = jnp.zeros((GROUP, bands * GROUP), jnp.float32)
    for c in range(bands):
        value = offset_ref[s, b, c] + (1.0 if b == c else 0.0)
        total = jnp.where(lane == row + c * GROUP, value, total)
    return total


def routes(me, footprint, depth, rows):
    shift = rows.bit_length() - 1
    relative = jnp.bitwise_xor(footprint, me)
    rel_y = relative & (rows - 1)
    rel_core = lax.shift_right_logical(relative, shift) & 1
    rel_x = lax.shift_right_logical(relative, shift + 1) & 1
    rel_z = lax.shift_right_logical(relative, shift + 2)
    chip = rel_x * rows + rel_y
    if rows == 2:
        core = lax.shift_right_logical(footprint, shift) & 1
        swap = jnp.logical_and(core == 1, jnp.logical_or(chip == 1, chip == 2))
        chip = jnp.where(swap, 3 - chip, chip)
        chip = jnp.bitwise_xor(chip, lax.shift_right_logical(chip, 1))
    return rel_z, rel_core * 2 * rows + chip


def resample(shape, chunk, offset_ref, x_ref, wait, code_cols, weights_ref, banded_ref, result_ref):
    bands, pixels = shape[:2]
    begin, end = chunk
    blocks = x_ref.shape[0]
    count = end - begin
    tiles = weights_ref.shape[0]
    high, low = [], []
    for s in range(2):
        exact = jnp.concatenate(
            [spread_mixing(offset_ref, s, b, bands) for b in range(begin, end)], axis=0
        )
        upper = exact.astype(jnp.bfloat16)
        high.append(upper)
        low.append((exact - upper.astype(jnp.float32)).astype(jnp.bfloat16))
    mixers = jnp.concatenate(high + low, axis=0)
    size = count * GROUP

    def one_group(g):
        here = pl.ds(pl.multiple_of(g * GROUP, GROUP), GROUP)
        stacked = jnp.concatenate(
            [x_ref[here, c * pixels : (c + 1) * pixels] for c in range(bands)], axis=0
        )
        mixed = dot(mixers, stacked)
        first = mixed[:size] + mixed[2 * size : 3 * size]
        second = mixed[size : 2 * size] + mixed[3 * size :]
        lanes = code_cols[here, :]
        choice = jnp.concatenate([lanes] * (pixels // 128), axis=1) > tiles - 0.5
        for b in range(count):
            part = slice(b * GROUP, (b + 1) * GROUP)
            banded_ref[b, here, :] = jnp.where(choice, second[part], first[part]).astype(
                jnp.bfloat16
            )

    step = UNROLL * GROUP
    for start in range(0, blocks, step):
        wait(start, step)
        for g in range(start // GROUP, (start + step) // GROUP):
            one_group(g)

    code = jnp.concatenate([code_cols[...]] * (pixels // 128), axis=1)
    pick = jnp.where(code > tiles - 0.5, code - tiles, code)
    for b in range(count):
        banded = banded_ref[b].astype(jnp.float32)
        total = None
        for t in range(tiles):
            part = dot(jnp.where(pick == t, banded, 0.0).astype(jnp.bfloat16), weights_ref[t])
            total = part if total is None else total + part
        result_ref[:, b * pixels : (b + 1) * pixels] = total.astype(jnp.bfloat16)


def pack(position, slots, peers, result_ref, out_refs, tags=None):
    blocks = result_ref.shape[0]
    height = out_refs[0].shape[0] // peers
    for core, ref in enumerate(out_refs):
        for k in range(peers):
            ids = lax.broadcasted_iota(jnp.int32, (slots, blocks), 0) + (core * peers + k) * slots
            chosen = one_hot(ids == position)
            start = k * height
            ref[start : start + slots, :] = dot(chosen, result_ref[...]).astype(jnp.bfloat16)
            if tags is not None:
                start, stop = start + slots, start + height
                ref[start:stop, :] = jnp.zeros((TAG_ROWS, ref.shape[1]), jnp.bfloat16)
                ref[start:stop, :slots] = lax.dot_general(
                    tags, chosen, (((1,), (1,)), ((), ())), preferred_element_type=jnp.float32
                ).astype(jnp.bfloat16)


def lead_kernel(shape, chunk, *refs):
    bands, pixels, rows, depth, slots, peers = shape
    ins, outs, scratch = refs[:8], refs[8:12], refs[12:]
    me_ref = ins[0]
    position_ref, code_cols = outs[2:]
    offset, x, foot, cell, pick, sensor, weights, banded_ref, result_ref, sems = scratch
    blocks = x.shape[0]
    tiles = weights.shape[0]
    step = UNROLL * GROUP
    small = [
        pltpu.make_async_copy(src, dst, sems.at[i])
        for i, (src, dst) in enumerate(
            ((ins[3], foot), (ins[4], cell), (ins[5], pick), (ins[6], sensor), (ins[1], offset))
        )
    ]
    matrices = pltpu.make_async_copy(ins[7], weights, sems.at[5])
    pieces = {
        start: pltpu.make_async_copy(
            ins[2].at[pl.ds(start, step), :], x.at[pl.ds(start, step), :], sems.at[6 + i]
        )
        for i, start in enumerate(range(0, blocks, step))
    }
    for copy in (*small, *pieces.values(), matrices):
        copy.start()
    for copy in small:
        copy.wait()

    code = pick[...] + tiles * sensor[...]
    code_cols[...] = jnp.broadcast_to(code.astype(jnp.float32), (128, blocks)).T

    place, group = routes(me_ref[0], foot[...], depth, rows)
    member = lax.broadcasted_iota(jnp.int32, (2 * peers, blocks), 0) == group
    member = member.astype(jnp.float32)
    earlier = lax.broadcasted_iota(jnp.int32, (blocks, blocks), 0) < lax.broadcasted_iota(
        jnp.int32, (blocks, blocks), 1
    )
    before = dot(member.astype(jnp.bfloat16), one_hot(earlier))
    rank = jnp.sum(member * before, axis=0, keepdims=True).astype(jnp.int32)
    position = group * slots + rank
    position_ref[...] = position
    line = lax.broadcasted_iota(jnp.int32, (TAG_ROWS, blocks), 0)
    tags = jnp.where(line == 0, cell[...] + 1, jnp.where(line == 1, place, 0))
    tags = tags.astype(jnp.float32).astype(jnp.bfloat16)

    def wait(start, size):
        pieces[start].wait()
        if start == 0:
            matrices.wait()

    resample(shape, chunk, offset, x, wait, code_cols, weights, banded_ref, result_ref)
    pack(position, slots, peers, result_ref, outs[:2], tags)


def follow_kernel(shape, chunk, *refs):
    slots, peers = shape[4:]
    offset_ref, x_ref, position_ref, code_cols, weights_ref = refs[:5]
    outs, (banded_ref, result_ref) = refs[5:7], refs[7:]
    resample(
        shape,
        chunk,
        offset_ref,
        x_ref,
        lambda start, size: None,
        code_cols,
        weights_ref,
        banded_ref,
        result_ref,
    )
    pack(position_ref[...], slots, peers, result_ref, outs)


def fold_kernel(picks, peers, mine_ref, crossed_ref, *outs):
    height = mine_ref.shape[0] // peers
    for parts, ref in zip(picks, outs):
        start = 0
        for k in parts:
            for source in (mine_ref, crossed_ref):
                ref[start : start + height, :] = source[k * height : (k + 1) * height, :]
                start += height


def join_kernel(peers, mine_ref, crossed_ref, arrived_ref, out_ref):
    height = mine_ref.shape[0] // peers
    out_ref[:height, :] = mine_ref[-height:, :]
    out_ref[height : 2 * height, :] = crossed_ref[-height:, :]
    out_ref[2 * height :, :] = arrived_ref[2 * height :, :]


def put(refs, planes):
    start = 0
    for ref in refs:
        ref[...] = planes[start : start + ref.shape[0]]
        start += ref.shape[0]


def merge_kernel(lead, slots, cells, parts, *refs):
    count = max(part[0] for part in parts) + 1
    rows = refs[:count]
    if lead:
        keep_ref, *sends, keys_ref = refs[count:]
    else:
        keys_ref, keep_ref, *sends = refs[count:]
    depth, columns = 2 * keep_ref.shape[0], keep_ref.shape[2]
    ids = lax.broadcasted_iota(jnp.int32, (depth * cells, slots), 0)
    total = None
    for i, (j, start) in enumerate(parts):
        stop = start + slots
        if lead:
            tag = rows[j][stop : stop + TAG_ROWS, :slots].astype(jnp.float32)
            cell, place = tag[0:1].astype(jnp.int32), tag[1:2].astype(jnp.int32)
            key = place * cells + cell - 1
            keys_ref[i] = key
        else:
            key = keys_ref[i]
        part = dot(one_hot(ids == key), rows[j][start:stop, :])
        total = part if total is None else total + part
    total = total.reshape(depth // 2, 2, cells, columns)
    keep_ref[...] = total[:, 0]
    put(sends, total[:, 1].astype(jnp.bfloat16))


def halve_kernel(count, *refs):
    kept_ref, arrived, keep_ref, sends = (
        refs[0],
        refs[1 : 1 + count],
        refs[1 + count],
        refs[2 + count :],
    )
    away = []
    start = 0
    for ref in arrived:
        for i in range(ref.shape[0]):
            plane = kept_ref[start] + ref[i].astype(jnp.float32)
            if start % 2 == 0:
                keep_ref[start // 2] = plane
            else:
                away.append(plane.astype(jnp.bfloat16)[None])
            start += 1
    put(sends, jnp.concatenate(away, axis=0))


def factor_kernel(bands, pixels, bin_ref, frac_ref, vol_ref, geo_ref, mask_ref, table_ref, brdf_ref, out_ref):
    rows = 8

    def some_rows(i, carry):
        here = pl.ds(pl.multiple_of(i * rows, rows), rows)
        for p in range(0, pixels, 128):
            at = (here, slice(p, p + 128))
            index, fraction = bin_ref[at], frac_ref[at]
            vol, geo = vol_ref[at], geo_ref[at]
            mask = mask_ref[at].astype(jnp.float32)
            for b in range(bands):
                line = jnp.broadcast_to(table_ref[b : b + 1, :], (rows, 128))
                lower = jnp.take_along_axis(line, index, axis=1)
                upper = jnp.take_along_axis(line, index + 1, axis=1)
                table_value = lower * (1.0 - fraction) + upper * fraction
                w0, w1, w2 = brdf_ref[b, 0], brdf_ref[b, 1], brdf_ref[b, 2]
                numerator = w0 + w1 * nadir_volume + w2 * nadir_geometric
                cfactor = numerator / (w0 + w1 * vol + w2 * geo)
                first = b * pixels + p
                out_ref[here, first : first + 128] = table_value * cfactor * mask
        return carry

    lax.fori_loop(0, out_ref.shape[0] // rows, some_rows, 0)


def total_kernel(kept_ref, arrived_ref, grid_ref):
    grid_ref[...] = kept_ref[0] + arrived_ref[0].astype(jnp.float32)


def finish_kernel(count, *refs):
    grids, (low_ref, high_ref, factor_ref, out_ref) = refs[:count], refs[count:]
    start = 0
    for grid_ref in grids:
        grid = grid_ref[...]
        here = slice(start, start + grid.shape[1])
        before = jnp.concatenate([low_ref[:, here], grid[:-1]], axis=0)
        after = jnp.concatenate([grid[1:], high_ref[:, here]], axis=0)
        smoothed = 0.25 * before + 0.5 * grid + 0.25 * after
        out_ref[:, here] = (smoothed * factor_ref[:, here]).astype(jnp.bfloat16)
        start = here.stop


def on_device(
    swath_blocks,
    footprint,
    cell_row,
    tile_pick,
    sensor,
    bandpass_offset,
    weight_tiles,
    lookup_table,
    lookup_bin,
    lookup_frac,
    brdf_params,
    vol_kernel,
    geo_kernel,
    clear_mask,
):
    tiles, rows = lax.axis_size("tile"), lax.axis_size("row")
    devices = tiles * rows
    blocks, width = swath_blocks.shape[2], swath_blocks.shape[3]
    bands = bandpass_offset.shape[1]
    pixels = width // bands
    cells = lookup_bin.shape[1]
    capacity = max(2, 3 * blocks // (2 * devices))
    depth = tiles // 4
    peers = 2 * rows
    slots = depth * capacity
    bits = dict(z=4 * rows, x=2 * rows, core=rows, y=1)

    def exchange(array, flip, other=None):
        flips = (flip, flip if other is None else other)
        pairs = [(i, i ^ flips[i // rows % 2]) for i in range(devices)]
        return lax.ppermute(array, ("tile", "row"), pairs)

    def chip_flip(k):
        return (k // rows) * bits["x"] + k % rows

    me = lax.axis_index("tile") * rows + lax.axis_index("row")
    smem = pl.BlockSpec(memory_space=pltpu.SMEM)
    hbm = pl.BlockSpec(memory_space=pltpu.HBM)
    shape = (bands, pixels, rows, depth, slots, peers)
    x = swath_blocks.reshape(blocks, width)
    table = jnp.pad(lookup_table, ((0, 0), (0, 128 - lookup_table.shape[1])))
    picks = ((1, 2),) if rows == 2 else tuple((k,) for k in range(1, peers))
    shared = {}
    chunks = [dict(hops=0) for _ in CHUNKS]

    def struct(*dims, dtype=jnp.bfloat16):
        return jax.ShapeDtypeStruct(dims, dtype)

    def send(i, after):
        begin, end = CHUNKS[i]
        columns = (end - begin) * pixels
        height = slots + (0 if i else TAG_ROWS)
        payload = [struct(peers * height, columns)] * 2
        work = [
            pltpu.VMEM((end - begin, blocks, pixels), jnp.bfloat16),
            pltpu.VMEM((blocks, columns), jnp.bfloat16),
        ]
        if i == 0:
            mine, cross, shared["position"], shared["codes"] = call(
                functools.partial(lead_kernel, shape, CHUNKS[i]),
                "lead",
                6,
                63,
                payload
                + [struct(1, blocks, dtype=jnp.int32), struct(blocks, 128, dtype=jnp.float32)],
                (
                    me.reshape(1).astype(jnp.int32),
                    bandpass_offset,
                    x,
                    footprint.reshape(1, blocks),
                    cell_row.reshape(1, blocks),
                    tile_pick.reshape(1, blocks),
                    sensor.reshape(1, blocks),
                    weight_tiles,
                ),
                after,
                in_specs=[smem] + [hbm] * 7,
                scratch_shapes=[
                    pltpu.SMEM(bandpass_offset.shape, jnp.float32),
                    pltpu.VMEM((blocks, width), jnp.bfloat16),
                    *[pltpu.VMEM((1, blocks), jnp.int32)] * 4,
                    pltpu.VMEM(weight_tiles.shape, jnp.bfloat16),
                    *work,
                    pltpu.SemaphoreType.DMA((6 + blocks // (UNROLL * GROUP),)),
                ],
            )
        else:
            mine, cross = call(
                functools.partial(follow_kernel, shape, CHUNKS[i]),
                "follow",
                2 + (end - begin),
                28,
                payload,
                (bandpass_offset, x, shared["position"], shared["codes"], weight_tiles),
                after,
                scalars=1,
                scratch_shapes=work,
            )
        chunks[i]["mine"], chunks[i]["crossed"] = mine, exchange(cross, bits["core"])
        return mine

    def fold(i, after):
        chunk = chunks[i]
        mine, crossed = chunk["mine"], chunk["crossed"]
        height, columns = mine.shape[0] // peers, mine.shape[1]
        outs = call(
            functools.partial(fold_kernel, picks, peers),
            "fold",
            0.3,
            16,
            [struct(2 * len(parts) * height, columns) for parts in picks],
            (mine, crossed),
            after,
        )
        if rows == 2:
            arrived = [exchange(outs[0], bits["y"], bits["x"])]
        else:
            arrived = [exchange(array, chip_flip(k + 1)) for k, array in enumerate(outs)]
        chunk["lists"] = [mine, crossed, *arrived]
        chunk["parts"] = [(0, 0), (1, 0)]
        for k in range(len(arrived)):
            chunk["parts"] += [(k + 2, 0), (k + 2, height)]
        return outs[0]

    def join(i, after):
        if rows != 2:
            return after
        chunk = chunks[i]
        arrived = chunk["lists"][2]
        both = call(
            functools.partial(join_kernel, peers),
            "join",
            0.3,
            16,
            struct(*arrived.shape),
            chunk["lists"],
            after,
        )
        chunk["lists"].append(exchange(both, bits["x"], bits["y"]))
        chunk["parts"] += [(3, k * (arrived.shape[0] // 4)) for k in range(4)]
        return both

    def forward(i, keep, sends):
        chunk = chunks[i]
        if i == len(chunks) - 1 and keep.shape[0] == 1:
            chunk["edges"] = edges(keep, sends[-1].reshape(cells, -1))
        chunk["keep"] = keep
        chunk["away"] = sends[-1]
        chunk["arrived"] = [exchange(array, bits["z"] << chunk["hops"]) for array in sends]
        chunk["hops"] += 1
        return sends[0]

    def pieces(hop, planes, columns):
        count = min(planes, SPLIT[min(hop, 1)])
        return [struct(planes // count, cells, columns)] * count

    def merge(i, after):
        arrays = chunks[i]["lists"]
        columns = arrays[0].shape[1]
        parts = chunks[i]["parts"]
        outs = [struct(depth // 2, cells, columns, dtype=jnp.float32)]
        outs += pieces(0, depth // 2, columns)
        if i == 0:
            outs.append(struct(2 * peers, 1, slots, dtype=jnp.int32))
        outs = call(
            functools.partial(merge_kernel, i == 0, slots, cells, parts),
            "merge",
            0.5 + 0.7 * columns / pixels,
            24,
            outs,
            (*arrays, *(() if i == 0 else (shared["keys"],))),
            after,
        )
        if i == 0:
            (*outs, shared["keys"]) = outs
        return forward(i, outs[0], outs[1:])

    def halve(i, after):
        if chunks[i]["keep"].shape[0] == 1:
            return after
        keep, arrived = chunks[i]["keep"], chunks[i]["arrived"]
        half, columns = keep.shape[0] // 2, keep.shape[2]
        outs = call(
            functools.partial(halve_kernel, len(arrived)),
            "halve",
            0.5,
            16,
            [
                struct(half, cells, columns, dtype=jnp.float32),
                *pieces(chunks[i]["hops"], half, columns),
            ],
            (keep, *arrived),
            after,
        )
        return forward(i, outs[0], outs[1:])

    def total(i, after):
        chunk = chunks[i]
        while chunk["keep"].shape[0] > 1:
            after = halve(i, after)
        chunk["grid"] = call(
            total_kernel,
            "total",
            0.3,
            16,
            struct(*chunk["keep"].shape[1:], dtype=jnp.float32),
            (chunk["keep"], *chunk["arrived"]),
            after,
        )
        return chunk["grid"]

    def edges(keep, away):
        early = chunks[:-1]
        def ends(array):
            return array[:1], array[-1:]

        parts = []
        for pick in (0, 1):
            kept = [ends(chunk["grid"])[pick] for chunk in early] + [ends(keep[0])[pick]]
            parts.append((jnp.concatenate(kept, axis=1), ends(away)[pick]))
        width_early = width - away.shape[1]
        hop = bits["z"] << (depth.bit_length() - 2)

        def beside(kept, coming):
            coming = jnp.pad(coming.astype(jnp.float32), ((0, 0), (width_early, 0)))
            return kept + coming

        if rows == 2:
            upper = lax.axis_index("row") == 0
            kept = jnp.where(upper, parts[1][0], parts[0][0])
            coming = jnp.where(upper, parts[1][1], parts[0][1])
            row = beside(exchange(kept, 1), exchange(coming, hop ^ 1))
            low, high = jnp.where(upper, 0.0, row), jnp.where(upper, row, 0.0)
        else:
            up = [(i, i + 1) for i in range(rows - 1)]
            down = [(i + 1, i) for i in range(rows - 1)]
            across = [(t * rows + r, (t * rows + r) ^ hop) for t in range(tiles) for r in range(rows)]
            low_pairs = [(i, j + 1) for i, j in across if j % rows < rows - 1]
            high_pairs = [(i, j - 1) for i, j in across if j % rows > 0]
            axes = ("tile", "row")
            low = beside(
                lax.ppermute(parts[1][0], "row", up), lax.ppermute(parts[1][1], axes, low_pairs)
            )
            high = beside(
                lax.ppermute(parts[0][0], "row", down), lax.ppermute(parts[0][1], axes, high_pairs)
            )
        return low, high

    def finish(i, after):
        low, high = chunks[-1]["edges"]
        return call(
            functools.partial(finish_kernel, len(chunks)),
            "finish",
            1,
            16,
            struct(cells, width),
            (*[chunk["grid"] for chunk in chunks], low, high, shared["factor"]),
            after,
        )

    def factors(i, after):
        shared["factor"] = call(
            functools.partial(factor_kernel, bands, pixels),
            "factor",
            3,
            16,
            struct(cells, width, dtype=jnp.float32),
            (
                lookup_bin[0],
                lookup_frac[0],
                vol_kernel[0],
                geo_kernel[0],
                clear_mask[0],
                table,
                brdf_params,
            ),
            after,
            in_specs=[pl.BlockSpec(memory_space=pltpu.VMEM)] * 6 + [smem],
        )
        return shared["factor"]

    steps = dict(s=send, k=fold, j=join, m=merge, h=halve, g=total, x=factors, f=finish)
    token = None
    for step in ORDER:
        token = steps[step[0]](int(step[1]), token)
    return token.reshape(1, cells, width)


def solution(mesh):
    in_specs = (
        P("tile", "row", None, None),
        P("tile", "row", None, None),
        P("tile", "row", None),
        P("tile", "row", None),
        P("tile", "row", None),
        P(),
        P(),
        P(),
        P("tile", "row", None),
        P("tile", "row", None),
        P(),
        P("tile", "row", None),
        P("tile", "row", None),
        P("tile", "row", None),
    )
    out_specs = P("tile", "row", None)
    return jax.shard_map(
        on_device, mesh=mesh, in_specs=in_specs, out_specs=out_specs, check_vma=False
    )
```
